128 devices in a mesh: ctx: 16 (over y, z), tp: 8 (over x, core).
Axes of the slice: x: 4, y: 4, z: 4, core: 2. Of those that a mesh axis runs over, the one named last changes fastest.
Arguments:
- projected: bfloat16 [8192, 5, 8192], P('ctx', None, 'tp'), may hold values from -6 to 6
- route: int32 [8192], P('ctx'), may hold values from 0 to 15, as said below
- contig_len: int32 [8], replicated, may hold values from 1 to 4096, 8192 in all
- mr_filter: float32 [128, 8192], P(None, 'tp'), may hold values from -0.5 to 0.5
- out_weight: bfloat16 [8192, 8192], P('tp'), may hold values from -0.0625 to 0.0625
- li_rate: float32 [16, 8192], P(None, 'tp'), may hold values from 6.1035157e-06 to 0.033
- li_residue: float32 [16, 8192], P(None, 'tp'), may hold values from -1.5 to 1.5
Outputs:
- mixed: bfloat16 [8192, 8192], P('ctx', 'tp')
The draws below stay inside these ranges and needn't reach their ends.
Inputs may be any that keep to these rules, and one draw needn't show every extreme that they name: `route`: of the 512 rows of one ctx index, at most 48 name the same context shard, and some do in every draw; every context shard is named by exactly 512 rows in all.
All inputs are finite; a program needn't handle non-finite values.
Results may differ from the reference program's by a relative error of at most 0.02.
Values may be sent and summed in bfloat16 or wider, within the bound.
No kernel may reach another device: no remote copies, remote signals or barrier semaphores. Data moves between devices by JAX's collectives and lax.ppermute only.
A program may use at most 192 MiB of HBM per device.

```python
import math
import jax
import jax.numpy as jnp
import numpy as np
from jax import lax

D = 8192
MR_LEN = 128
ORDER = 16
CONTIGS = 8
TOK_DEV = 512
TOKENS = 8192
N_CTX = 16
N_TP = 8


def draw_route(key, part):
    ctx_count = N_CTX
    base_count = TOK_DEV // N_CTX
    half_base = base_count // 2
    order_key, amount_key, row_key = jax.random.split(key, 3)
    shift_order = jax.random.permutation(order_key, ctx_count).astype(jnp.int32)
    amounts = jax.random.randint(amount_key, (ctx_count // 2,), 0, half_base + 1).astype(jnp.int32)
    amounts = amounts.at[0].set(half_base)
    weight_vec = jnp.full((ctx_count,), base_count, jnp.int32)
    weight_vec = weight_vec.at[shift_order[0::2]].add(amounts)
    weight_vec = weight_vec.at[shift_order[1::2]].add(-amounts)
    loaders = jnp.arange(ctx_count, dtype=jnp.int32)
    shift_table = (loaders[None, :] - loaders[:, None]) % ctx_count
    counts = jnp.take(weight_vec, shift_table)
    run_ends = jnp.cumsum(counts, axis=1).astype(jnp.int32)
    row_ids = jnp.arange(TOK_DEV, dtype=jnp.int32)
    targets = jnp.sum((run_ends[:, None, :] <= row_ids[None, :, None]).astype(jnp.int32), axis=2)
    row_keys = jax.random.split(row_key, ctx_count)
    shuffles = jax.vmap(lambda one_key: jax.random.permutation(one_key, TOK_DEV))(row_keys).astype(jnp.int32)
    shuffled = jnp.take_along_axis(targets, shuffles, axis=1)
    return shuffled.reshape(ctx_count * TOK_DEV).astype(jnp.int32)


def level_of(stream_key, dims, cuts, least, largest):
    def one(axis_at, parts):
        draws = jax.random.uniform(jax.random.fold_in(jax.random.fold_in(stream_key, 6), axis_at), (parts,), jnp.float32, least / len(cuts), largest / len(cuts))
        return jnp.repeat(jnp.exp(draws), dims[axis_at] // parts).reshape((-1,) + (1,) * (len(dims) - axis_at - 1))

    gain = one(*cuts[0])
    for cut in cuts[1:]:
        gain = gain * one(*cut)
    return gain


def split_up(number_of, total, most, slope):
    portions = [(1 << 20) // math.isqrt(standing ** slope) + 1 for standing in range(2, number_of + 1)]
    spare, given = total - most - (number_of - 1), [1] * (number_of - 1)
    while spare > 0:
        movable = [i for i in range(number_of - 1) if given[i] < most]
        pool, left = sum([portions[i] for i in movable]), spare
        for i in movable:
            extra = min(most - given[i], max(1, left * portions[i] // pool), spare)
            given[i] = given[i] + extra
            spare = spare - extra
    return np.array([most] + given)


def uneven(own_key, amount, total, most, slope):
    if amount == 2:
        one = jax.random.randint(own_key, (), max(1, total - most), min(most, total - 1) + 1)
        return jnp.stack([one, total - one])
    lengths = jnp.asarray(split_up(amount, total, most, slope), jnp.int32)
    twos = (amount - 1) // 2
    giver, sink = lengths[1:1 + 2 * twos:2], lengths[2:2 + 2 * twos:2]
    margin = jnp.minimum(giver - 1, most - sink)
    shifted = jax.random.randint(jax.random.fold_in(own_key, 1), (twos,), 0, 1 << 20) % (margin + 1)
    lengths = lengths.at[1:1 + 2 * twos:2].set(giver - shifted).at[2:2 + 2 * twos:2].set(sink + shifted)
    return lengths[jax.random.permutation(jax.random.fold_in(own_key, 2), amount)]


def bell_draw(rng, extent, width, reach, pieces=(), kind=jnp.bfloat16):
    array = jax.random.normal(rng, extent, jnp.float32) * width
    if len(pieces) > 0:
        array = level_of(rng, extent, pieces, -0.22, 0.18) * array
    return jnp.clip(array, min=-reach, max=reach).astype(kind)


def setup_inputs(seed: int = 0) -> dict:
    key_list = jax.random.split(jax.random.key(seed), 8)
    return {
        "projected": bell_draw(key_list[0], (TOKENS, 5, D), 1.0, 6.0, ((0, 16), (2, 8))),
        "route": draw_route(jax.random.fold_in(key_list[7], 71), 0),
        "contig_len": uneven(key_list[2], CONTIGS, TOKENS, TOKENS // 2, 2).astype(jnp.int32),
        "mr_filter": bell_draw(key_list[3], (MR_LEN, D), MR_LEN ** -0.5, 0.5, ((1, 8),), jnp.float32),
        "out_weight": bell_draw(key_list[4], (D, D), D ** -0.5, 0.0625, ((0, 8),)),
        "li_rate": jnp.clip(jnp.exp(math.log(0.033) - 8.595398 * jax.random.uniform(key_list[5], (ORDER, D), jnp.float32) ** level_of(key_list[5], (ORDER, D), ((1, 8),), -0.2, 0.2)), 6.10351571594947e-06, 0.033),
        "li_residue": bell_draw(key_list[6], (ORDER, D), ORDER ** -0.5, 1.5, ((1, 8),), jnp.float32),
    }


def tap_filter(padded, taps, rows):
    tap_total = taps.shape[0]

    def add_tap(tap_id, total):
        tap_index = jnp.asarray(tap_id).astype(jnp.int32)
        start = (tap_total - 1 - tap_index).astype(jnp.int32)
        window = lax.dynamic_slice_in_dim(padded, start, rows, 0)
        tap_row = lax.dynamic_index_in_dim(taps, tap_index, 0, keepdims=False)
        return total + tap_row[None, :] * window
    init = jnp.zeros((rows, padded.shape[1]), padded.dtype)
    return lax.fori_loop(0, tap_total, add_tap, init)

def reference(projected, route, contig_len, mr_filter, out_weight, li_rate, li_residue):
    tokens = projected.shape[0]
    channels = projected.shape[2]
    peer_ids = jnp.arange(N_CTX, dtype=jnp.int32)
    one_hot = (route[:, None] == peer_ids[None, :]).astype(jnp.int32)
    before = (jnp.cumsum(one_hot, axis=0).astype(jnp.int32) - one_hot) * one_hot
    row_rank = lax.optimization_barrier(jnp.sum(before, axis=1)).astype(jnp.int32)
    position = (route * TOK_DEV + row_rank).astype(jnp.int32)
    ordered = jnp.zeros_like(projected).at[position].set(projected)
    u_mr = ordered[:, 1].astype(jnp.float32) * ordered[:, 2].astype(jnp.float32)
    padded = jnp.concatenate([jnp.zeros((MR_LEN - 1, channels), jnp.float32), u_mr], axis=0)
    filtered = tap_filter(padded, mr_filter, tokens)
    gated = (ordered[:, 0].astype(jnp.float32) * filtered).astype(jnp.bfloat16)
    group_width = channels // N_TP
    mr_out = jnp.zeros((tokens, channels), jnp.float32)
    for group_id in range(N_TP):
        low = group_id * group_width
        piece = jnp.dot(gated[:, low:low + group_width], out_weight[low:low + group_width], preferred_element_type=jnp.float32)
        rounded = lax.optimization_barrier(piece.astype(jnp.bfloat16))
        mr_out = mr_out + rounded.astype(jnp.float32)
    starts = (jnp.cumsum(contig_len) - contig_len).astype(jnp.int32)
    seq_pos = jnp.arange(tokens, dtype=jnp.int32)
    is_start = jnp.any(seq_pos[:, None] == starts[None, :], axis=1)
    keep_mask = jnp.where(is_start, 0.0, 1.0).astype(jnp.float32)
    u_li = ordered[:, 4].astype(jnp.float32) * mr_out
    decays = jnp.exp(-li_rate)
    mode_weight = li_residue * jnp.sqrt(-jnp.expm1(-2.0 * li_rate))

    def advance(carry_state, inputs):
        keep_row, u_row = inputs
        carry_state = decays * carry_state * keep_row + u_row[None, :]
        return (carry_state, lax.optimization_barrier(jnp.sum(mode_weight * carry_state, axis=0)))
    _, li_out = lax.scan(advance, jnp.zeros((ORDER, channels), jnp.float32), (keep_mask, u_li))
    y_seq = (ordered[:, 3].astype(jnp.float32) * li_out).astype(jnp.bfloat16)
    return y_seq[position]
```

```python
import functools

import jax
import jax.numpy as jnp
import ml_dtypes
import numpy as np
from jax import lax
from jax.experimental import pallas as pl
from jax.experimental.pallas import tpu as pltpu
from jax.sharding import PartitionSpec as P

f32 = jnp.float32
bf16 = jnp.bfloat16
i32 = jnp.int32
SEGS = 8
CHUNKS = 2
ORDER = 16


def dot(a, b):
    return jnp.dot(a, b, preferred_element_type=f32)


def dot_t(a, b):
    return lax.dot_general(a, b, (((0,), (0,)), ((), ())), preferred_element_type=f32)


def iota(shape, dim):
    return lax.broadcasted_iota(i32, shape, dim)


def ones_where(mask):
    return jnp.where(mask, 1.0, 0.0).astype(bf16)


def params(mib=48):
    return pltpu.CompilerParams(vmem_limit_bytes=mib * 2**20)


def cost(flops, nbytes):
    return pl.CostEstimate(flops=int(flops), bytes_accessed=int(nbytes), transcendentals=0)


def whole(shape):
    return pl.BlockSpec(shape, lambda *_: (0,) * len(shape))


def cols(shape):
    return pl.BlockSpec(shape, lambda j, *_: (0,) * (len(shape) - 1) + (j,))


def send_matrix(route, slots, slot_count):
    rows = route.shape[1]
    peers = slots // slot_count
    hot = iota((peers, rows), 0) == route
    earlier = ones_where(iota((rows, rows), 0) < iota((rows, rows), 1))
    rank = dot(ones_where(hot), earlier)
    rank = jnp.sum(jnp.where(hot, rank, 0.0), axis=0, keepdims=True)
    slot = route * slot_count + rank.astype(i32)
    return ones_where(iota((slots, rows), 0) == slot)


def place_matrix(every_route, me, slots, slot_count):
    peers, rows = every_route.shape
    count = jnp.sum(jnp.where(every_route == me, 1.0, 0.0), axis=1, keepdims=True)
    lane = iota((peers, slots), 1)
    low = iota((peers, slots), 0) * slot_count
    mine = (lane >= low) & (lane < low + slot_count)
    before = jnp.sum(jnp.where(lane >= low + slot_count, count, 0.0), axis=0, keepdims=True)
    held = jnp.sum(jnp.where(mine, count, 0.0), axis=0, keepdims=True)
    within = jnp.sum(jnp.where(mine, (lane - low).astype(f32), 0.0), axis=0, keepdims=True)
    at = jnp.where(within < held, before + within, -1.0).astype(i32)
    return ones_where(iota((rows, slots), 0) == at)


def pack_product(planes, route, first, second, slot_count, peers, tile=512):
    _, rows, channels = planes.shape
    slots = peers * slot_count

    def body(route_ref, a_ref, *rest):
        out_ref, hot_ref = rest[-2:]

        @pl.when(pl.program_id(0) == 0)
        def _():
            hot_ref[...] = send_matrix(route_ref[...], slots, slot_count)

        x = a_ref[0]
        if second is not None:
            x = (x.astype(f32) * rest[0][0].astype(f32)).astype(bf16)
        out_ref[...] = dot(hot_ref[...], x).astype(bf16)

    picks = [first] if second is None else [first, second]
    return pl.pallas_call(
        body,
        grid=(channels // tile,),
        in_specs=[whole((1, rows))]
        + [pl.BlockSpec((1, rows, tile), functools.partial(lambda s, j: (s, 0, j), s)) for s in picks],
        out_specs=cols((slots, tile)),
        out_shape=jax.ShapeDtypeStruct((slots, channels), bf16),
        scratch_shapes=[pltpu.VMEM((slots, rows), bf16)],
        compiler_params=params(),
        cost_estimate=cost(2 * slots * rows * channels, 2 * (rows * len(picks) + slots) * channels),
        name="pack",
    )(route, *([planes] * len(picks)))


def unpack(received, every_route, me, slot_count, tile=512):
    slots, channels = received.shape
    rows = every_route.shape[1]

    def body(me_ref, every_ref, in_ref, out_ref, hot_ref):
        @pl.when(pl.program_id(0) == 0)
        def _():
            hot_ref[...] = place_matrix(every_ref[...], me_ref[0], slots, slot_count)

        out_ref[...] = dot(hot_ref[...], in_ref[...]).astype(bf16)

    return pl.pallas_call(
        body,
        grid_spec=pltpu.PrefetchScalarGridSpec(
            num_scalar_prefetch=1,
            grid=(channels // tile,),
            in_specs=[whole(every_route.shape), cols((slots, tile))],
            out_specs=cols((rows, tile)),
            scratch_shapes=[pltpu.VMEM((rows, slots), bf16)],
        ),
        out_shape=jax.ShapeDtypeStruct((rows, channels), bf16),
        compiler_params=params(),
        cost_estimate=cost(2 * slots * rows * channels, 2 * (rows + slots) * channels),
        name="unpack",
    )(me, every_route, received)


def finish(returned, planes, plane, route, slot_count):
    slots, width = returned[0].shape
    _, rows, channels = planes.shape

    def body(route_ref, gate_ref, *rest):
        out_ref = rest[-1]
        hot = send_matrix(route_ref[...], slots, slot_count)
        for h in range(len(returned)):
            at = slice(h * width, (h + 1) * width)
            out_ref[:, at] = (gate_ref[0, :, at].astype(f32) * dot_t(hot, rest[h][...])).astype(bf16)

    return pl.pallas_call(
        body,
        grid=(1,),
        in_specs=[whole((1, rows)), pl.BlockSpec((1, rows, channels), lambda j: (plane, 0, 0))]
        + [whole((slots, width))] * len(returned),
        out_specs=whole((rows, channels)),
        out_shape=jax.ShapeDtypeStruct((rows, channels), bf16),
        compiler_params=params(),
        cost_estimate=cost(2 * slots * rows * channels, 2 * (2 * rows + slots) * channels),
        name="finish",
    )(route, planes, *returned)


def two_parts(table):
    high = table.astype(ml_dtypes.bfloat16)
    return high, (table - high.astype(np.float64)).astype(ml_dtypes.bfloat16)


def dft_tables(taps):
    points = 2 * taps
    k = np.arange(taps)[:, None].astype(np.float64)
    t = np.arange(points)[None, :].astype(np.float64)
    forward = np.concatenate(
        [np.cos(2 * np.pi * k * t / points), np.cos(np.pi * t), -np.sin(2 * np.pi * k[1:] * t / points)]
    )
    inverse = forward.T[taps:] * (2.0 / points)
    inverse[:, 0] *= 0.5
    inverse[:, taps] *= 0.5
    return np.concatenate(two_parts(forward)), np.concatenate(two_parts(inverse))


def forward_dft(table, x):
    both = dot(table, x)
    half = both.shape[0] // 2
    return both[:half] + both[half:]


def inverse_dft(table, y):
    half = table.shape[0] // 2
    high = y.astype(bf16)
    low = (y - high.astype(f32)).astype(bf16)
    both = dot(table, high)
    return both[:half] + both[half:] + dot(table[:half], low)


def through_filter(spectrum, filter_ref, inverse_table):
    taps = spectrum.shape[0] // 2
    a, b = spectrum[:taps], spectrum[taps:]
    re, im, re_last = filter_ref[0], filter_ref[1], filter_ref[2]
    return inverse_dft(inverse_table, jnp.concatenate([a * re - b * im, a * im + b * re_last]))


def filter_spectrum(mr_filter, forward, tile=512):
    taps, channels = mr_filter.shape

    def body(taps_ref, fwd_ref, out_ref):
        fwd = fwd_ref[:, :taps]
        x = taps_ref[...]
        high = x.astype(bf16)
        low = (x - high.astype(f32)).astype(bf16)
        h = forward_dft(fwd, high) + dot(fwd[: 2 * taps], low)
        first = iota((taps, tile), 0) == 0
        out_ref[0] = h[:taps]
        out_ref[1] = jnp.where(first, 0.0, h[taps:])
        out_ref[2] = jnp.where(first, h[taps:], h[:taps])

    return pl.pallas_call(
        body,
        grid=(channels // tile,),
        in_specs=[cols((taps, tile)), whole(forward.shape)],
        out_specs=cols((3, taps, tile)),
        out_shape=jax.ShapeDtypeStruct((3, taps, channels), f32),
        compiler_params=params(),
        cost_estimate=cost(6 * 2 * taps * taps * channels, 16 * taps * channels),
        name="spectrum",
    )(mr_filter, forward)


def filter_rows(u, spectrum, forward, inverse, tile=512):
    rows, channels = u.shape
    taps = spectrum.shape[1]

    def body(u_ref, h_ref, fwd_ref, inv_ref, out_ref):
        for b in range(rows // taps):
            at = slice(b * taps, (b + 1) * taps)
            if b == 0:
                x = forward_dft(fwd_ref[:, taps:], u_ref[at])
            else:
                x = forward_dft(fwd_ref[...], u_ref[(b - 1) * taps : (b + 1) * taps])
            out_ref[at] = through_filter(x, h_ref, inv_ref[...])

    return pl.pallas_call(
        body,
        grid=(channels // tile,),
        in_specs=[cols((rows, tile)), cols((3, taps, tile)), whole(forward.shape), whole(inverse.shape)],
        out_specs=cols((rows, tile)),
        out_shape=jax.ShapeDtypeStruct((rows, channels), f32),
        compiler_params=params(),
        cost_estimate=cost(14 * taps * rows * channels, 8 * rows * channels),
        name="taps",
    )(u, spectrum, forward, inverse)


def gate(received, every_route, me, filtered, rim, spectrum, forward, inverse, slot_count, tile=512):
    slots, channels = received.shape
    rows = every_route.shape[1]
    taps = spectrum.shape[1]

    def body(me_ref, every_ref, in_ref, filt_ref, rim_ref, h_ref, fwd_ref, inv_ref, out_ref, hot_ref):
        @pl.when(pl.program_id(0) == 0)
        def _():
            hot_ref[...] = place_matrix(every_ref[...], me_ref[0], slots, slot_count)

        q = dot(hot_ref[...], in_ref[...])
        early = through_filter(forward_dft(fwd_ref[:, :taps], rim_ref[...]), h_ref, inv_ref[...])
        out_ref[:taps] = (q[:taps] * (filt_ref[:taps] + early)).astype(bf16)
        out_ref[taps:] = (q[taps:] * filt_ref[taps:]).astype(bf16)

    return pl.pallas_call(
        body,
        grid_spec=pltpu.PrefetchScalarGridSpec(
            num_scalar_prefetch=1,
            grid=(channels // tile,),
            in_specs=[
                whole(every_route.shape),
                cols((slots, tile)),
                cols((rows, tile)),
                cols((taps, tile)),
                cols((3, taps, tile)),
                whole(forward.shape),
                whole(inverse.shape),
            ],
            out_specs=cols((rows, tile)),
            scratch_shapes=[pltpu.VMEM((rows, slots), bf16)],
        ),
        out_shape=jax.ShapeDtypeStruct((rows, channels), bf16),
        compiler_params=params(),
        cost_estimate=cost(2 * slots * rows * channels, (6 * rows + 2 * slots) * channels),
        name="gate",
    )(me, every_route, received, filtered, rim, spectrum, forward, inverse)


def project(tasks, chunk, blocks, own, other, weight, other_weights, adds, out_type, tile=256):
    rows, depth = own.shape
    width = depth // CHUNKS
    steps = width // tile
    count = len(tasks)

    def body(blocks_ref, own_ref, other_ref, *rest):
        for n, (_, low, take) in enumerate(tasks):
            at = slice(low, low + take)
            total = dot(own_ref[at], rest[2 * n][...]) + dot(other_ref[at], rest[2 * n + 1][...])
            if adds:
                total = total + rest[2 * count + n][...].astype(f32)
            rest[2 * count + len(adds) + n][...] = total.astype(out_type)

    specs = [whole((rows, depth))] * 2
    operands = [own, other]
    for dx, _, _ in tasks:
        specs.append(
            pl.BlockSpec(
                (depth, tile),
                functools.partial(lambda d, j, b: (0, (b[d] * CHUNKS + chunk) * steps + j), dx),
            )
        )
        specs.append(pl.BlockSpec((depth, tile), lambda j, b: (0, chunk * steps + j)))
        operands += [weight, other_weights[dx]]
    for arrived in adds:
        specs.append(cols((arrived.shape[0], tile)))
        operands.append(arrived)
    total_rows = sum(take for _, _, take in tasks)
    return pl.pallas_call(
        body,
        grid_spec=pltpu.PrefetchScalarGridSpec(
            num_scalar_prefetch=1,
            grid=(steps,),
            in_specs=specs,
            out_specs=[cols((take, tile)) for _, _, take in tasks],
        ),
        out_shape=[jax.ShapeDtypeStruct((take, width), out_type) for _, _, take in tasks],
        compiler_params=params(),
        cost_estimate=cost(
            4 * depth * width * total_rows, 4 * depth * width * count + 4 * rows * depth + 4 * total_rows * width
        ),
        name="project",
    )(blocks, *operands)


def end_states(chunk, table, own, arrived, k_li, last, coef):
    rows, width = own.shape
    half = rows // 2
    steps = rows // SEGS

    def body(table_ref, own_ref, a0_ref, a1_ref, b0_ref, b1_ref, k_ref, last_ref, coef_ref, u_ref, seg_ref, end_ref):
        top = own_ref[:half] + a0_ref[...].astype(f32) + a1_ref[...].astype(f32)
        top = top * k_ref[:half].astype(f32)
        bottom = own_ref[half:] + b0_ref[...].astype(f32) + b1_ref[...].astype(f32)
        bottom = bottom * k_ref[half:].astype(f32)
        for cb in range(width // 128):
            lanes = slice(cb * 128, (cb + 1) * 128)
            u_ref[cb, :half] = top[:, lanes]
            u_ref[cb, half:] = bottom[:, lanes]
            decay = [jnp.broadcast_to(coef_ref[0, n : n + 1, lanes], (SEGS, 128)) for n in range(ORDER)]

            def step(t, state):
                u = u_ref[cb, pl.ds(t, SEGS, stride=steps), :] * last_ref[pl.ds(t, SEGS, stride=steps), :]
                return tuple(d * s + u for d, s in zip(decay, state))

            state = lax.fori_loop(0, steps, step, (jnp.zeros((SEGS, 128), f32),) * ORDER, unroll=4)
            for n in range(ORDER):
                seg_ref[cb, n * SEGS : (n + 1) * SEGS] = state[n]
            total = jnp.zeros((ORDER, 128), f32)
            for s in range(SEGS):
                keep = jnp.where(table_ref[s] == 0, coef_ref[1, :, lanes], 0.0)
                total = keep * total + seg_ref[cb, pl.ds(s, ORDER, stride=SEGS), :]
            end_ref[:, lanes] = total

    piece = whole((half, width))
    return pl.pallas_call(
        body,
        grid_spec=pltpu.PrefetchScalarGridSpec(
            num_scalar_prefetch=1,
            grid=(1,),
            in_specs=[
                whole((rows, width)),
                piece,
                piece,
                piece,
                piece,
                pl.BlockSpec((rows, width), lambda j, b: (0, chunk)),
                whole(last.shape),
                pl.BlockSpec((4, ORDER, width), lambda j, b: (0, 0, chunk)),
            ],
            out_specs=[
                whole((width // 128, rows, 128)),
                whole((width // 128, ORDER * SEGS, 128)),
                whole((ORDER, width)),
            ],
        ),
        out_shape=[
            jax.ShapeDtypeStruct((width // 128, rows, 128), f32),
            jax.ShapeDtypeStruct((width // 128, ORDER * SEGS, 128), f32),
            jax.ShapeDtypeStruct((ORDER, width), f32),
        ],
        compiler_params=params(),
        cost_estimate=cost(2e9, 8 * rows * width),
        name="ends",
    )(table, own, *arrived, k_li, last, coef)


def recur(chunk, table, ends, segs, u, keep, coef, every_route, slot_count):
    blocks, rows, _ = u.shape
    width = 128 * blocks
    steps = rows // SEGS
    peers = every_route.shape[0]
    slots = peers * slot_count

    def body(table_ref, ends_ref, seg_ref, u_ref, keep_ref, coef_ref, every_ref, out_ref, in_ref, li_ref):
        me = table_ref[SEGS + peers]

        def hop(j, carry):
            return jnp.where(table_ref[SEGS + j] == 0, coef_ref[2], 0.0) * carry + ends_ref[j]

        carry = lax.fori_loop(0, me, hop, jnp.zeros((ORDER, width), f32))
        for cb in range(blocks):
            lanes = slice(cb * 128, (cb + 1) * 128)
            enter = carry[:, lanes]
            for s in range(SEGS):
                in_ref[cb, pl.ds(s, ORDER, stride=SEGS), :] = enter
                fade = jnp.where(table_ref[s] == 0, coef_ref[1, :, lanes], 0.0)
                enter = fade * enter + seg_ref[cb, pl.ds(s, ORDER, stride=SEGS), :]
            decay = [jnp.broadcast_to(coef_ref[0, n : n + 1, lanes], (SEGS, 128)) for n in range(ORDER)]
            weigh = [jnp.broadcast_to(coef_ref[3, n : n + 1, lanes], (SEGS, 128)) for n in range(ORDER)]
            state = tuple(in_ref[cb, n * SEGS : (n + 1) * SEGS] for n in range(ORDER))

            def step(t, state):
                u = u_ref[cb, pl.ds(t, SEGS, stride=steps), :]
                kept = keep_ref[pl.ds(t, SEGS, stride=steps), :]
                state = tuple((d * s) * kept + u for d, s in zip(decay, state))
                terms = [w * s for w, s in zip(weigh, state)]
                while len(terms) > 1:
                    terms = [a + b for a, b in zip(terms[::2], terms[1::2])]
                li_ref[cb, pl.ds(t, SEGS, stride=steps), :] = terms[0]
                return state

            lax.fori_loop(0, steps, step, state, unroll=4)
        hot = place_matrix(every_ref[...], me, slots, slot_count)
        li = jnp.concatenate([li_ref[cb].astype(bf16) for cb in range(blocks)], axis=1)
        out_ref[...] = dot_t(hot, li).astype(bf16)

    return pl.pallas_call(
        body,
        grid_spec=pltpu.PrefetchScalarGridSpec(
            num_scalar_prefetch=1,
            grid=(1,),
            in_specs=[
                whole(ends.shape),
                whole(segs.shape),
                whole(u.shape),
                whole(keep.shape),
                pl.BlockSpec((4, ORDER, width), lambda j, b: (0, 0, chunk)),
                whole(every_route.shape),
            ],
            out_specs=whole((slots, width)),
            scratch_shapes=[pltpu.VMEM(segs.shape, f32), pltpu.VMEM(u.shape, f32)],
        ),
        out_shape=jax.ShapeDtypeStruct((slots, width), bf16),
        compiler_params=params(),
        cost_estimate=cost(4e9, 8 * rows * width),
        name="recur",
    )(table, ends, segs, u, keep, coef, every_route)


def along_x(shard, dx, dcore=0):
    count = lax.axis_size("tp") // 2
    pairs = [
        (2 * x + c, 2 * ((x + dx) % count) + (c + dcore) % 2) for x in range(count) for c in range(2)
    ]
    return lax.ppermute(shard, "tp", pairs)


def swap(shard):
    return lax.all_to_all(shard, "ctx", split_axis=0, concat_axis=0, tiled=True)


def together(*arrays):
    return lax.optimization_barrier(arrays)


def on_device(projected, route, contig_len, mr_filter, out_weight, li_rate, li_residue):
    rows, _, channels = projected.shape
    peers = lax.axis_size("ctx")
    slot_count = 3 * rows // (2 * peers)
    taps = mr_filter.shape[0]
    half = rows // 2
    me = lax.axis_index("ctx").astype(i32)
    tp = lax.axis_index("tp").astype(i32)
    chip, core = tp // 2, tp % 2
    chips = lax.axis_size("tp") // 2
    planes = jnp.transpose(projected, (1, 0, 2))
    route_row = route.reshape(1, rows)
    me_row = me.reshape(1)
    forward, inverse = (jnp.asarray(t) for t in dft_tables(taps))

    every_route = lax.all_gather(route, "ctx", axis=0, tiled=False)
    packed_kv = pack_product(planes, route_row, 1, 2, slot_count, peers)
    packed_kv, every_route = together(packed_kv, every_route)
    got_kv = swap(packed_kv)
    packed_q = pack_product(planes, route_row, 0, None, slot_count, peers)
    packed_k = pack_product(planes, route_row, 4, None, slot_count, peers)

    order = jnp.arange(contig_len.shape[0], dtype=i32)
    starts = jnp.sum(jnp.where(order[:, None] < order[None, :], contig_len[:, None], 0), axis=0)
    span = rows // SEGS
    here = me * rows + jnp.arange(rows, dtype=i32)
    seg_last = here - here % span + (span - 1)
    keep = jnp.where(jnp.any(here[:, None] == starts[None, :], axis=1), 0.0, 1.0).astype(f32)
    last = jnp.where(
        jnp.any((starts[None, :] > here[:, None]) & (starts[None, :] <= seg_last[:, None]), axis=1), 0.0, 1.0
    ).astype(f32)
    keep = jnp.broadcast_to(keep[:, None], (rows, 128))
    last = jnp.broadcast_to(last[:, None], (rows, 128))
    seg_ids = me * SEGS + jnp.arange(SEGS, dtype=i32)
    seg_has = jnp.any(seg_ids[:, None] == (starts // span)[None, :], axis=1)
    dev_has = jnp.any(jnp.arange(peers, dtype=i32)[:, None] == (starts // rows)[None, :], axis=1)
    table = jnp.concatenate([seg_has.astype(i32), dev_has.astype(i32), me_row])
    mode_weight = li_residue * jnp.sqrt(-jnp.expm1(-2.0 * li_rate))
    coef = jnp.stack([jnp.exp(-li_rate), jnp.exp(-li_rate * span), jnp.exp(-li_rate * rows), mode_weight])
    spectrum = filter_spectrum(mr_filter, forward)

    blocks = jnp.stack([2 * ((chip + d) % chips) + core for d in range(chips)]).astype(i32)
    depth = out_weight.shape[0]
    other_weights = [
        along_x(lax.dynamic_slice(out_weight, (0, (2 * ((chip + d) % chips) + 1 - core) * depth), (depth, depth)), 0, 1)
        for d in range(chips)
    ]

    got_kv, packed_q = together(got_kv, packed_q)
    got_q = swap(packed_q)
    u_mr = unpack(got_kv, every_route, me_row, slot_count)
    rim = lax.ppermute(u_mr[rows - taps :], "ctx", [(i, i + 1) for i in range(peers - 1)])
    filtered = filter_rows(u_mr, spectrum, forward, inverse)
    got_q, packed_k = together(got_q, packed_k)
    gated = gate(got_q, every_route, me_row, filtered, rim, spectrum, forward, inverse, slot_count)
    got_k = swap(packed_k)
    other = along_x(gated, 0, 1)
    mm = functools.partial(project, blocks=blocks, own=gated, other=other, weight=out_weight, other_weights=other_weights)

    k_li = None
    returned = []
    for h in range(CHUNKS):
        far_a, far_b = mm([(2, 0, half), (2, half, half)], h, adds=[], out_type=bf16)
        pass_a, pass_b = along_x(far_a, 1), along_x(far_b, -1)
        up_b, down_a = mm([(1, half, half), (3, 0, half)], h, adds=[], out_type=bf16)
        from_low_b, from_high_a = along_x(up_b, 1), along_x(down_a, -1)
        [mine] = mm([(0, 0, rows)], h, adds=[], out_type=f32)
        up_a, down_b = mm([(1, 0, half), (3, half, half)], h, adds=[pass_a, pass_b], out_type=bf16)
        from_low_a, from_high_b = along_x(up_a, 1), along_x(down_b, -1)
        if k_li is None:
            k_li = unpack(got_k, every_route, me_row, slot_count)
        u, segs, end = end_states(
            h, table, mine, [from_low_a, from_high_a, from_low_b, from_high_b], k_li, last, coef
        )
        ends = lax.all_gather(end, "ctx", axis=0, tiled=False)
        homeward = recur(h, table, ends, segs, u, keep, coef, every_route, slot_count)
        returned.append(swap(homeward))
    return finish(returned, planes, 3, route_row, slot_count)


def solution(mesh):
    return jax.shard_map(
        on_device,
        mesh=mesh,
        in_specs=(
            P("ctx", None, "tp"),
            P("ctx"),
            P(),
            P(None, "tp"),
            P("tp", None),
            P(None, "tp"),
            P(None, "tp"),
        ),
        out_specs=P("ctx", "tp"),
        check_vma=False,
    )
```

```python
import functools

import jax
import jax.numpy as jnp
import ml_dtypes
import numpy as np
from jax import lax
from jax.experimental import pallas as pl
from jax.experimental.pallas import tpu as pltpu
from jax.sharding import PartitionSpec as P

f32 = jnp.float32
bf16 = jnp.bfloat16
i32 = jnp.int32
SEGS = 8
ORDER = 16
EMPTY = 64.0
MIB = 48


def dot(a, b):
    return jnp.dot(a, b, preferred_element_type=f32)


def iota(shape, dim):
    return lax.broadcasted_iota(i32, shape, dim)


def ones_where(mask):
    return jnp.where(mask, 1.0, 0.0).astype(bf16)


def params(mib=MIB):
    return pltpu.CompilerParams(vmem_limit_bytes=mib * 2**20)


def cost(flops, nbytes):
    return pl.CostEstimate(flops=int(flops) // 10, bytes_accessed=int(nbytes) // 10, transcendentals=0)


def whole(shape):
    return pl.BlockSpec(shape, lambda *_: (0,) * len(shape))


def cols(shape):
    return pl.BlockSpec(shape, lambda j, *_: (0,) * (len(shape) - 1) + (j,))


def leading(shape):
    return pl.BlockSpec(shape, lambda j, *_: (j,) + (0,) * (len(shape) - 1))


def as_column(row):
    return jnp.transpose(jnp.broadcast_to(row.astype(f32), (128, row.shape[1])))[:, :1].astype(i32)


def send_slots(route, peers, slot_count):
    rows = route.shape[1]
    hot = iota((peers, rows), 0) == route
    earlier = ones_where(iota((rows, rows), 0) < iota((rows, rows), 1))
    rank = dot(ones_where(hot), earlier)
    rank = jnp.sum(jnp.where(hot, rank, 0.0), axis=0, keepdims=True)
    return route * slot_count + rank.astype(i32)


def place_rows(count, slots):
    peers = count.shape[0]
    per = slots // peers
    lane = iota((peers, slots), 1)
    low = iota((peers, slots), 0) * per
    mine = (lane >= low) & (lane < low + per)
    before = jnp.sum(jnp.where(lane >= low + per, count, 0.0), axis=0, keepdims=True)
    held = jnp.sum(jnp.where(mine, count, 0.0), axis=0, keepdims=True)
    within = jnp.sum(jnp.where(mine, (lane - low).astype(f32), 0.0), axis=0, keepdims=True)
    return jnp.where(within < held, before + within, -1.0).astype(i32)


def pack_product(planes, route, first, second, slot_count, peers, tile=256):
    _, rows, channels = planes.shape
    slots = peers * slot_count

    def body(route_ref, a_ref, b_ref, out_ref, hot_ref, fill_ref):
        @pl.when(pl.program_id(0) == 0)
        def _():
            hot = ones_where(iota((slots, rows), 0) == send_slots(route_ref[...], peers, slot_count))
            hot_ref[...] = hot
            fill_ref[...] = EMPTY * (1.0 - dot(hot, jnp.ones((rows, 128), bf16)))

        x = (a_ref[0].astype(f32) * b_ref[0].astype(f32)).astype(bf16)
        out_ref[...] = (dot(hot_ref[...], x) + fill_ref[:, :1]).astype(bf16)

    return pl.pallas_call(
        body,
        grid=(channels // tile,),
        in_specs=[whole((1, rows))]
        + [pl.BlockSpec((1, rows, tile), functools.partial(lambda s, j: (s, 0, j), s)) for s in (first, second)],
        out_specs=cols((slots, tile)),
        out_shape=jax.ShapeDtypeStruct((slots, channels), bf16),
        scratch_shapes=[pltpu.VMEM((slots, rows), bf16), pltpu.VMEM((slots, 128), f32)],
        compiler_params=params(),
        cost_estimate=cost(2 * slots * rows * channels, 2 * (2 * rows + slots) * channels),
        name="pack_kv",
    )(route, planes, planes)


def pack_two(planes, route, first, second, slot_count, peers, tile=512):
    _, rows, channels = planes.shape
    slots = peers * slot_count

    def body(route_ref, a_ref, b_ref, out_a_ref, out_b_ref, back_ref, hot_ref):
        @pl.when(pl.program_id(0) == 0)
        def _():
            slot = send_slots(route_ref[...], peers, slot_count)
            hot_ref[...] = ones_where(iota((slots, rows), 0) == slot)
            back_ref[...] = ones_where(iota((rows, slots), 1) == as_column(slot))

        out_a_ref[...] = dot(hot_ref[...], a_ref[0]).astype(bf16)
        out_b_ref[...] = dot(hot_ref[...], b_ref[0]).astype(bf16)

    return pl.pallas_call(
        body,
        grid=(channels // tile,),
        in_specs=[whole((1, rows))]
        + [pl.BlockSpec((1, rows, tile), functools.partial(lambda s, j: (s, 0, j), s)) for s in (first, second)],
        out_specs=[cols((slots, tile)), cols((slots, tile)), whole((rows, slots))],
        out_shape=[
            jax.ShapeDtypeStruct((slots, channels), bf16),
            jax.ShapeDtypeStruct((slots, channels), bf16),
            jax.ShapeDtypeStruct((rows, slots), bf16),
        ],
        scratch_shapes=[pltpu.VMEM((slots, rows), bf16)],
        compiler_params=params(),
        cost_estimate=cost(4 * slots * rows * channels, 4 * (rows + slots) * channels),
        name="pack_two",
    )(route, planes, planes)


def place_matrices(received, rows, slot_count, peers):
    slots = received.shape[0]

    def body(in_ref, to_ref, steps_ref, back_ref):
        used = ones_where(in_ref[...].astype(f32) < 0.75 * EMPTY)
        lane = iota((peers, slots), 1)
        low = iota((peers, slots), 0) * slot_count
        at = place_rows(dot(ones_where((lane >= low) & (lane < low + slot_count)), used)[:, :1], slots)
        to_ref[...] = ones_where(iota((rows, slots), 0) == at)
        span = rows // SEGS
        at = jnp.where(at < 0, at, (at % span) * SEGS + at // span)
        steps_ref[...] = ones_where(iota((rows, slots), 0) == at)
        back_ref[...] = ones_where(iota((slots, rows), 1) == as_column(at))

    return pl.pallas_call(
        body,
        grid=(1,),
        in_specs=[pl.BlockSpec((slots, 128), lambda j: (0, 0))],
        out_specs=[whole((rows, slots)), whole((rows, slots)), whole((slots, rows))],
        out_shape=[
            jax.ShapeDtypeStruct((rows, slots), bf16),
            jax.ShapeDtypeStruct((rows, slots), bf16),
            jax.ShapeDtypeStruct((slots, rows), bf16),
        ],
        compiler_params=params(),
        cost_estimate=cost(1e6, 6 * rows * slots),
        name="place",
    )(received)


def unpack(received, to_rows, tile=512):
    slots, channels = received.shape
    rows = to_rows.shape[0]

    def body(hot_ref, in_ref, out_ref):
        out_ref[...] = dot(hot_ref[...], in_ref[...]).astype(bf16)

    return pl.pallas_call(
        body,
        grid=(channels // tile,),
        in_specs=[whole(to_rows.shape), cols((slots, tile))],
        out_specs=cols((rows, tile)),
        out_shape=jax.ShapeDtypeStruct((rows, channels), bf16),
        compiler_params=params(),
        cost_estimate=cost(2 * slots * rows * channels, 2 * (rows + slots) * channels),
        name="unpack",
    )(to_rows, received)


def finish(returned, planes, plane, back, tile=512):
    slots, channels = returned.shape
    _, rows, _ = planes.shape

    def body(back_ref, gate_ref, in_ref, out_ref):
        out_ref[...] = (gate_ref[0].astype(f32) * dot(back_ref[...], in_ref[...])).astype(bf16)

    return pl.pallas_call(
        body,
        grid=(channels // tile,),
        in_specs=[
            whole((rows, slots)),
            pl.BlockSpec((1, rows, tile), lambda j: (plane, 0, j)),
            cols((slots, tile)),
        ],
        out_specs=cols((rows, tile)),
        out_shape=jax.ShapeDtypeStruct((rows, channels), bf16),
        compiler_params=params(),
        cost_estimate=cost(2 * slots * rows * channels, 2 * (2 * rows + slots) * channels),
        name="finish",
    )(back, planes, returned)


def two_parts(table):
    high = table.astype(ml_dtypes.bfloat16)
    return high, (table - high.astype(np.float64)).astype(ml_dtypes.bfloat16)


def dft_tables(taps):
    points = 2 * taps
    k = np.arange(taps)[:, None].astype(np.float64)
    t = np.arange(points)[None, :].astype(np.float64)
    forward = np.concatenate(
        [np.cos(2 * np.pi * k * t / points), np.cos(np.pi * t), -np.sin(2 * np.pi * k[1:] * t / points)]
    )
    inverse = forward.T[taps:] * (2.0 / points)
    inverse[:, 0] *= 0.5
    inverse[:, taps] *= 0.5
    return np.concatenate(two_parts(forward)), np.concatenate(two_parts(inverse))


def side_by_side(rows):
    p = np.arange(rows)
    t = (p % SEGS) * (rows // SEGS) + p // SEGS
    return (t[:, None] == p[None, :]).astype(ml_dtypes.bfloat16)


def forward_dft(table, x):
    both = dot(table, x)
    half = both.shape[0] // 2
    return both[:half] + both[half:]


def inverse_dft(table, y):
    half = table.shape[0] // 2
    high = y.astype(bf16)
    low = (y - high.astype(f32)).astype(bf16)
    both = dot(table, high)
    return both[:half] + both[half:] + dot(table[:half], low)


def through_filter(spectrum, filter_ref, inverse_table):
    taps = spectrum.shape[0] // 2
    a, b = spectrum[:taps], spectrum[taps:]
    re, im, re_last = filter_ref[0], filter_ref[1], filter_ref[2]
    return inverse_dft(inverse_table, jnp.concatenate([a * re - b * im, a * im + b * re_last]))


def filter_spectrum(mr_filter, forward, tile=512):
    taps, channels = mr_filter.shape

    def body(taps_ref, fwd_ref, out_ref):
        fwd = fwd_ref[:, :taps]
        x = taps_ref[...]
        high = x.astype(bf16)
        low = (x - high.astype(f32)).astype(bf16)
        h = forward_dft(fwd, high) + dot(fwd[: 2 * taps], low)
        first = iota((taps, tile), 0) == 0
        out_ref[0] = h[:taps]
        out_ref[1] = jnp.where(first, 0.0, h[taps:])
        out_ref[2] = jnp.where(first, h[taps:], h[:taps])

    return pl.pallas_call(
        body,
        grid=(channels // tile,),
        in_specs=[cols((taps, tile)), whole(forward.shape)],
        out_specs=cols((3, taps, tile)),
        out_shape=jax.ShapeDtypeStruct((3, taps, channels), f32),
        compiler_params=params(),
        cost_estimate=cost(6 * 2 * taps * taps * channels, 16 * taps * channels),
        name="spectrum",
    )(mr_filter, forward)


def filter_rows(u, spectrum, forward, inverse, tile=512):
    rows, channels = u.shape
    taps = spectrum.shape[1]

    def body(u_ref, h_ref, fwd_ref, inv_ref, out_ref):
        for b in range(rows // taps):
            if b == 0:
                x = forward_dft(fwd_ref[:, taps:], u_ref[:taps])
            else:
                x = forward_dft(fwd_ref[...], u_ref[(b - 1) * taps : (b + 1) * taps])
            out_ref[b * taps : (b + 1) * taps] = through_filter(x, h_ref, inv_ref[...])

    return pl.pallas_call(
        body,
        grid=(channels // tile,),
        in_specs=[cols((rows, tile)), cols((3, taps, tile)), whole(forward.shape), whole(inverse.shape)],
        out_specs=cols((rows, tile)),
        out_shape=jax.ShapeDtypeStruct((rows, channels), f32),
        compiler_params=params(),
        cost_estimate=cost(14 * taps * rows * channels, 8 * rows * channels),
        name="taps",
    )(u, spectrum, forward, inverse)


def gate(received, to_rows, filtered, rim, spectrum, forward, inverse, beside, tile=512):
    slots, channels = received.shape
    rows = to_rows.shape[0]
    taps = spectrum.shape[1]

    def body(hot_ref, in_ref, filt_ref, rim_ref, h_ref, fwd_ref, inv_ref, beside_ref, out_ref):
        q = dot(hot_ref[...], in_ref[...])
        early = through_filter(forward_dft(fwd_ref[:, :taps], rim_ref[...]), h_ref, inv_ref[...])
        first = (q[:taps] * (filt_ref[:taps] + early)).astype(bf16)
        rest = (q[taps:] * filt_ref[taps:]).astype(bf16)
        out_ref[...] = dot(beside_ref[...], jnp.concatenate([first, rest])).astype(bf16)

    return pl.pallas_call(
        body,
        grid=(channels // tile,),
        in_specs=[
            whole(to_rows.shape),
            cols((slots, tile)),
            cols((rows, tile)),
            cols((taps, tile)),
            cols((3, taps, tile)),
            whole(forward.shape),
            whole(inverse.shape),
            whole((rows, rows)),
        ],
        out_specs=cols((rows, tile)),
        out_shape=jax.ShapeDtypeStruct((rows, channels), bf16),
        compiler_params=params(),
        cost_estimate=cost(2 * slots * rows * channels, (6 * rows + 2 * slots) * channels),
        name="gate",
    )(to_rows, received, filtered, rim, spectrum, forward, inverse, beside)


def project(tasks, blocks, own, other, weight, other_weight, tile=512):
    rows, depth = own.shape
    width = depth
    steps = width // tile
    adds = [add for _, _, _, add, _ in tasks if add is not None]
    shapes = [jax.ShapeDtypeStruct((take, width), kind) for _, _, splits, _, kind in tasks for take in splits]

    def body(blocks_ref, own_ref, other_ref, *rest):
        arrived = iter(rest[2 * len(tasks) : 2 * len(tasks) + len(adds)])
        outs = iter(rest[2 * len(tasks) + len(adds) :])
        for n, (_, low, splits, add, kind) in enumerate(tasks):
            at = slice(low, low + sum(splits))
            total = dot(own_ref[at], rest[2 * n][...]) + dot(other_ref[at], rest[2 * n + 1][...])
            if add is not None:
                total = total + next(arrived)[...].astype(f32)
            start = 0
            for take in splits:
                next(outs)[...] = total[start : start + take].astype(kind)
                start += take

    specs = [whole((rows, depth))] * 2
    operands = [own, other]
    for dx, *_ in tasks:
        spec = pl.BlockSpec(
            (depth, tile), functools.partial(lambda d, j, b: (0, b[d] * steps + j), dx)
        )
        specs += [spec, spec]
        operands += [weight, other_weight]
    for add in adds:
        specs.append(cols((add.shape[0], tile)))
        operands.append(add)
    total_rows = sum(shape.shape[0] for shape in shapes)
    return pl.pallas_call(
        body,
        grid_spec=pltpu.PrefetchScalarGridSpec(
            num_scalar_prefetch=1,
            grid=(steps,),
            in_specs=specs,
            out_specs=[cols((shape.shape[0], tile)) for shape in shapes],
        ),
        out_shape=shapes,
        compiler_params=params(),
        cost_estimate=cost(
            4 * depth * width * total_rows, 4 * depth * width * len(tasks) + 4 * rows * depth + 4 * total_rows * width
        ),
        name="project",
    )(blocks, *operands)


def rows_of(t):
    return pl.ds(pl.multiple_of(t * SEGS, SEGS), SEGS)


def spread(ref, which, lanes):
    return [jnp.broadcast_to(ref[which, n : n + 1, lanes], (SEGS, 128)) for n in range(ORDER)]


def total_of(terms):
    while len(terms) > 1:
        terms = [a + b for a, b in zip(terms[::2], terms[1::2])]
    return terms[0]


def end_states(table, own, arrived, k_li, last, coef, peers, tile=256):
    rows, width = own.shape
    half = rows // 2
    blocks = tile // 128

    def body(table_ref, own_ref, a0_ref, a1_ref, b0_ref, b1_ref, k_ref, last_ref, coef_ref, u_ref, seg_ref, end_ref):
        top = own_ref[:half] + a0_ref[...].astype(f32) + a1_ref[...].astype(f32)
        top = top * k_ref[:half].astype(f32)
        bottom = own_ref[half:] + b0_ref[...].astype(f32) + b1_ref[...].astype(f32)
        bottom = bottom * k_ref[half:].astype(f32)
        for cb in range(blocks):
            lanes = slice(cb * 128, (cb + 1) * 128)
            u_ref[cb, :half] = top[:, lanes]
            u_ref[cb, half:] = bottom[:, lanes]
        for cb in range(blocks):
            lanes = slice(cb * 128, (cb + 1) * 128)
            decay = spread(coef_ref, 0, lanes)

            def step(t, state):
                u = u_ref[cb, rows_of(t), :] * last_ref[rows_of(t), :]
                return tuple(d * s + u for d, s in zip(decay, state))

            state = lax.fori_loop(0, rows // SEGS, step, (jnp.zeros((SEGS, 128), f32),) * ORDER, unroll=8)
            for n in range(ORDER):
                seg_ref[cb, n * SEGS : (n + 1) * SEGS] = state[n]
            total = jnp.zeros((ORDER, 128), f32)
            for s in range(SEGS):
                keep = jnp.where(table_ref[s] == 0, coef_ref[1, :, lanes], 0.0)
                total = keep * total + seg_ref[cb, pl.ds(s, ORDER, stride=SEGS), :]
            for p in range(peers):
                end_ref[p * ORDER : (p + 1) * ORDER, lanes] = total.astype(bf16)

    return pl.pallas_call(
        body,
        grid_spec=pltpu.PrefetchScalarGridSpec(
            num_scalar_prefetch=1,
            grid=(width // tile,),
            in_specs=[
                cols((rows, tile)),
                cols((half, tile)),
                cols((half, tile)),
                cols((half, tile)),
                cols((half, tile)),
                cols((rows, tile)),
                whole(last.shape),
                cols((4, ORDER, tile)),
            ],
            out_specs=[
                leading((blocks, rows, 128)),
                leading((blocks, ORDER * SEGS, 128)),
                cols((peers * ORDER, tile)),
            ],
        ),
        out_shape=[
            jax.ShapeDtypeStruct((width // 128, rows, 128), f32),
            jax.ShapeDtypeStruct((width // 128, ORDER * SEGS, 128), f32),
            jax.ShapeDtypeStruct((peers * ORDER, width), bf16),
        ],
        compiler_params=params(),
        cost_estimate=cost(4e9, 12 * rows * width),
        name="ends",
    )(table, own, *arrived, k_li, last, coef)


def recur(table, segs, u, keep, coef, step_blocks=2):
    count, rows, _ = u.shape

    def body(table_ref, seg_ref, u_ref, keep_ref, coef_ref, li_ref, in_ref):
        for cb in range(step_blocks):
            lanes = slice(cb * 128, (cb + 1) * 128)
            enter = jnp.zeros((ORDER, 128), f32)
            for s in range(SEGS):
                in_ref[pl.ds(s, ORDER, stride=SEGS), :] = enter
                fade = jnp.where(table_ref[s] == 0, coef_ref[1, :, lanes], 0.0)
                enter = fade * enter + seg_ref[cb, pl.ds(s, ORDER, stride=SEGS), :]
            decay, weigh = spread(coef_ref, 0, lanes), spread(coef_ref, 3, lanes)

            def step(t, state):
                u, kept = u_ref[cb, rows_of(t), :], keep_ref[rows_of(t), :]
                state = tuple((d * s) * kept + u for d, s in zip(decay, state))
                li_ref[cb, rows_of(t), :] = total_of([w * s for w, s in zip(weigh, state)])
                return state

            state = tuple(in_ref[n * SEGS : (n + 1) * SEGS] for n in range(ORDER))
            lax.fori_loop(0, rows // SEGS, step, state, unroll=8)

    return pl.pallas_call(
        body,
        grid_spec=pltpu.PrefetchScalarGridSpec(
            num_scalar_prefetch=1,
            grid=(count // step_blocks,),
            in_specs=[
                leading((step_blocks, ORDER * SEGS, 128)),
                leading((step_blocks, rows, 128)),
                whole(keep.shape),
                cols((4, ORDER, step_blocks * 128)),
            ],
            out_specs=leading((step_blocks, rows, 128)),
            scratch_shapes=[pltpu.VMEM((ORDER * SEGS, 128), f32)],
        ),
        out_shape=jax.ShapeDtypeStruct(u.shape, f32),
        compiler_params=params(),
        cost_estimate=cost(8e9, 8 * count * rows * 128),
        name="recur",
    )(table, segs, u, keep, coef)


def carry_in(table, ends, li, unbroken, coef, back, peers, step_blocks=2):
    count, rows, _ = li.shape
    slots = back.shape[0]
    tile = step_blocks * 128

    def body(table_ref, ends_ref, li_ref, unbroken_ref, coef_ref, back_ref, out_ref, in_ref, sum_ref):
        def hop(j, carry):
            return jnp.where(table_ref[SEGS + j] == 0, coef_ref[2], 0.0) * carry + ends_ref[j].astype(f32)

        carry = lax.fori_loop(0, table_ref[SEGS + peers], hop, jnp.zeros((ORDER, tile), f32))
        for cb in range(step_blocks):
            lanes = slice(cb * 128, (cb + 1) * 128)
            enter = carry[:, lanes] * coef_ref[3, :, lanes]
            for s in range(SEGS):
                in_ref[pl.ds(s, ORDER, stride=SEGS), :] = enter
                enter = coef_ref[1, :, lanes] * enter
            decay = spread(coef_ref, 0, lanes)

            def step(t, state):
                state = tuple(d * s for d, s in zip(decay, state))
                more = total_of(list(state)) * unbroken_ref[rows_of(t), :]
                sum_ref[rows_of(t), lanes] = li_ref[cb, rows_of(t), :] + more
                return state

            state = tuple(in_ref[n * SEGS : (n + 1) * SEGS] for n in range(ORDER))
            lax.fori_loop(0, rows // SEGS, step, state, unroll=8)
        out_ref[...] = dot(back_ref[...], sum_ref[...].astype(bf16)).astype(bf16)

    return pl.pallas_call(
        body,
        grid_spec=pltpu.PrefetchScalarGridSpec(
            num_scalar_prefetch=1,
            grid=(count // step_blocks,),
            in_specs=[
                cols((peers, ORDER, tile)),
                leading((step_blocks, rows, 128)),
                whole(unbroken.shape),
                cols((4, ORDER, tile)),
                whole(back.shape),
            ],
            out_specs=cols((slots, tile)),
            scratch_shapes=[pltpu.VMEM((ORDER * SEGS, 128), f32), pltpu.VMEM((rows, tile), f32)],
        ),
        out_shape=jax.ShapeDtypeStruct((slots, count * 128), bf16),
        compiler_params=params(),
        cost_estimate=cost(4e9, 8 * count * rows * 128),
        name="carry",
    )(table, ends, li, unbroken, coef, back)


def along_x(shard, dx, dcore=0):
    count = lax.axis_size("tp") // 2
    pairs = [
        (2 * x + c, 2 * ((x + dx) % count) + (c + dcore) % 2) for x in range(count) for c in range(2)
    ]
    return lax.ppermute(shard, "tp", pairs)


def lane_mask(hit):
    return jnp.broadcast_to(jnp.where(hit, 0.0, 1.0).astype(f32)[:, None], (hit.shape[0], 128))


def swap(shard):
    return lax.all_to_all(shard, "ctx", split_axis=0, concat_axis=0, tiled=True)


def together(*arrays):
    return lax.optimization_barrier(arrays)


def on_device(projected, route, contig_len, mr_filter, out_weight, li_rate, li_residue):
    rows, _, channels = projected.shape
    peers = lax.axis_size("ctx")
    slot_count = 3 * rows // (2 * peers)
    taps = mr_filter.shape[0]
    half = rows // 2
    me = lax.axis_index("ctx").astype(i32)
    tp = lax.axis_index("tp").astype(i32)
    chip, core = tp // 2, tp % 2
    chips = lax.axis_size("tp") // 2
    planes = jnp.transpose(projected, (1, 0, 2))
    route_row = route.reshape(1, rows)
    me_row = me.reshape(1)
    span = rows // SEGS
    forward, inverse = (jnp.asarray(t) for t in dft_tables(taps))
    beside = jnp.asarray(side_by_side(rows))

    packed_kv = pack_product(planes, route_row, 1, 2, slot_count, peers)
    packed_kv, other_source = together(packed_kv, out_weight)
    other_weight = along_x(other_source, 0, 1)
    got_kv = swap(packed_kv)
    packed_q, packed_k, to_loader = pack_two(planes, route_row, 0, 4, slot_count, peers)

    order = jnp.arange(contig_len.shape[0], dtype=i32)
    starts = jnp.sum(jnp.where(order[:, None] < order[None, :], contig_len[:, None], 0), axis=0)
    here = me * rows + jnp.arange(SEGS, dtype=i32)[None, :] * span + jnp.arange(span, dtype=i32)[:, None]
    here = here.reshape(rows, 1)
    seg_last = here - here % span + (span - 1)
    seen, behind = starts[None, :] <= here, starts[None, :] > here
    keep = lane_mask(jnp.any(starts[None, :] == here, axis=1))
    last = lane_mask(jnp.any(behind & (starts[None, :] <= seg_last), axis=1))
    unbroken = lane_mask(jnp.any(seen & (starts[None, :] >= me * rows), axis=1))
    seg_ids = me * SEGS + jnp.arange(SEGS, dtype=i32)
    seg_has = jnp.any(seg_ids[:, None] == (starts // span)[None, :], axis=1)
    dev_has = jnp.any(jnp.arange(peers, dtype=i32)[:, None] == (starts // rows)[None, :], axis=1)
    table = jnp.concatenate([seg_has.astype(i32), dev_has.astype(i32), me_row])
    mode_weight = li_residue * jnp.sqrt(-jnp.expm1(-2.0 * li_rate))
    coef = jnp.stack([jnp.exp(-li_rate), jnp.exp(-li_rate * span), jnp.exp(-li_rate * rows), mode_weight])
    spectrum = filter_spectrum(mr_filter, forward)

    blocks = jnp.stack([2 * ((chip + d) % chips) + core for d in range(chips)]).astype(i32)

    got_kv, packed_q, coef, spectrum = together(got_kv, packed_q, coef, spectrum)
    got_q = swap(packed_q)
    to_rows, to_steps, to_slots = place_matrices(got_kv, rows, slot_count, peers)
    u_mr = unpack(got_kv, to_rows)
    rim = lax.ppermute(u_mr[rows - taps :], "ctx", [(i, i + 1) for i in range(peers - 1)])
    filtered = filter_rows(u_mr, spectrum, forward, inverse)
    got_q, filtered, packed_k = together(got_q, filtered, packed_k)
    got_k = swap(packed_k)
    gated = gate(got_q, to_rows, filtered, rim, spectrum, forward, inverse, beside)
    other = along_x(gated, 0, 1)
    mm = functools.partial(project, own=gated, weight=out_weight, other_weight=other_weight)
    far_a, far_b = mm([(2, 0, (half, half), None, bf16)], blocks, other=other)
    blocks, far_a, far_b = together(blocks, far_a, far_b)
    pass_a, pass_b = along_x(far_a, 1), along_x(far_b, -1)
    up_b, down_a = mm([(1, half, (half,), None, bf16), (3, 0, (half,), None, bf16)], blocks, other=other)
    up_b, down_a, blocks = together(up_b, down_a, blocks)
    from_low_b, from_high_a = along_x(up_b, 1), along_x(down_a, -1)
    [mine] = mm([(0, 0, (rows,), None, f32)], blocks, other=other)
    got_k, pass_a, pass_b, mine = together(got_k, pass_a, pass_b, mine)
    k_li = unpack(got_k, to_steps)
    up_a, down_b = mm([(1, 0, (half,), pass_a, bf16), (3, half, (half,), pass_b, bf16)], blocks, other=other)
    from_low_a, from_high_b = along_x(up_a, 1), along_x(down_b, -1)
    u, segs, end = end_states(
        table, mine, [from_low_a, from_high_a, from_low_b, from_high_b], k_li, last, coef, peers
    )
    ends = swap(end).reshape(peers, ORDER, channels)
    li = recur(table, segs, u, keep, coef)
    returned = swap(carry_in(table, ends, li, unbroken, coef, to_slots, peers))
    return finish(returned, planes, 3, to_loader)


def solution(mesh):
    return jax.shard_map(
        on_device,
        mesh=mesh,
        in_specs=(
            P("ctx", None, "tp"),
            P("ctx"),
            P(),
            P(None, "tp"),
            P("tp", None),
            P(None, "tp"),
            P(None, "tp"),
        ),
        out_specs=P("ctx", "tp"),
        check_vma=False,
    )
```

```python
import functools

import jax
import jax.numpy as jnp
import ml_dtypes
import numpy as np
from jax import lax
from jax.experimental import pallas as pl
from jax.experimental.pallas import tpu as pltpu
from jax.sharding import PartitionSpec as P

f32 = jnp.float32
bf16 = jnp.bfloat16
i32 = jnp.int32
SEGS = 8
ORDER = 16
EMPTY = 64.0
MIB = 48


def dot(a, b):
    return jnp.dot(a, b, preferred_element_type=f32)


def iota(shape, dim):
    return lax.broadcasted_iota(i32, shape, dim)


def ones_where(mask):
    return jnp.where(mask, 1.0, 0.0).astype(bf16)


def params(mib=MIB):
    return pltpu.CompilerParams(vmem_limit_bytes=mib * 2**20)


def cost(flops, nbytes):
    return pl.CostEstimate(flops=int(flops) // 10, bytes_accessed=int(nbytes) // 10, transcendentals=0)


def whole(shape):
    return pl.BlockSpec(shape, lambda *_: (0,) * len(shape))


def cols(shape):
    return pl.BlockSpec(shape, lambda j, *_: (0,) * (len(shape) - 1) + (j,))


def leading(shape):
    return pl.BlockSpec(shape, lambda j, *_: (j,) + (0,) * (len(shape) - 1))


def as_column(row):
    return jnp.transpose(jnp.broadcast_to(row.astype(f32), (128, row.shape[1])))[:, :1].astype(i32)


def send_slots(route, peers, slot_count):
    rows = route.shape[1]
    hot = iota((peers, rows), 0) == route
    earlier = ones_where(iota((rows, rows), 0) < iota((rows, rows), 1))
    rank = dot(ones_where(hot), earlier)
    rank = jnp.sum(jnp.where(hot, rank, 0.0), axis=0, keepdims=True)
    return route * slot_count + rank.astype(i32)


def place_rows(count, slots):
    peers = count.shape[0]
    per = slots // peers
    lane = iota((peers, slots), 1)
    low = iota((peers, slots), 0) * per
    mine = (lane >= low) & (lane < low + per)
    before = jnp.sum(jnp.where(lane >= low + per, count, 0.0), axis=0, keepdims=True)
    held = jnp.sum(jnp.where(mine, count, 0.0), axis=0, keepdims=True)
    within = jnp.sum(jnp.where(mine, (lane - low).astype(f32), 0.0), axis=0, keepdims=True)
    return jnp.where(within < held, before + within, -1.0).astype(i32)


def pack_product(planes, route, first, second, slot_count, peers, tile=512):
    _, rows, channels = planes.shape
    slots = peers * slot_count

    def body(route_ref, a_ref, b_ref, out_ref, hot_ref, fill_ref):
        @pl.when(pl.program_id(0) == 0)
        def _():
            hot = ones_where(iota((slots, rows), 0) == send_slots(route_ref[...], peers, slot_count))
            hot_ref[...] = hot
            fill_ref[...] = EMPTY * (1.0 - dot(hot, jnp.ones((rows, 128), bf16)))

        x = (a_ref[0].astype(f32) * b_ref[0].astype(f32)).astype(bf16)
        out_ref[...] = (dot(hot_ref[...], x) + fill_ref[:, :1]).astype(bf16)

    return pl.pallas_call(
        body,
        grid=(channels // tile,),
        in_specs=[whole((1, rows))]
        + [pl.BlockSpec((1, rows, tile), functools.partial(lambda s, j: (s, 0, j), s)) for s in (first, second)],
        out_specs=cols((slots, tile)),
        out_shape=jax.ShapeDtypeStruct((slots, channels), bf16),
        scratch_shapes=[pltpu.VMEM((slots, rows), bf16), pltpu.VMEM((slots, 128), f32)],
        compiler_params=params(),
        cost_estimate=cost(2 * slots * rows * channels, 2 * (2 * rows + slots) * channels),
        name="pack_kv",
    )(route, planes, planes)


def pack_two(planes, route, first, second, slot_count, peers, tile=512):
    _, rows, channels = planes.shape
    slots = peers * slot_count

    def body(route_ref, a_ref, b_ref, out_a_ref, out_b_ref, back_ref, hot_ref):
        @pl.when(pl.program_id(0) == 0)
        def _():
            slot = send_slots(route_ref[...], peers, slot_count)
            hot_ref[...] = ones_where(iota((slots, rows), 0) == slot)
            back_ref[...] = ones_where(iota((rows, slots), 1) == as_column(slot))

        out_a_ref[...] = dot(hot_ref[...], a_ref[0]).astype(bf16)
        out_b_ref[...] = dot(hot_ref[...], b_ref[0]).astype(bf16)

    return pl.pallas_call(
        body,
        grid=(channels // tile,),
        in_specs=[whole((1, rows))]
        + [pl.BlockSpec((1, rows, tile), functools.partial(lambda s, j: (s, 0, j), s)) for s in (first, second)],
        out_specs=[cols((slots, tile)), cols((slots, tile)), whole((rows, slots))],
        out_shape=[
            jax.ShapeDtypeStruct((slots, channels), bf16),
            jax.ShapeDtypeStruct((slots, channels), bf16),
            jax.ShapeDtypeStruct((rows, slots), bf16),
        ],
        scratch_shapes=[pltpu.VMEM((slots, rows), bf16)],
        compiler_params=params(),
        cost_estimate=cost(4 * slots * rows * channels, 4 * (rows + slots) * channels),
        name="pack_two",
    )(route, planes, planes)


def place_matrices(received, rows, slot_count, peers):
    slots = received.shape[0]

    def body(in_ref, to_ref, steps_ref, back_ref):
        used = ones_where(in_ref[...].astype(f32) < 0.75 * EMPTY)
        lane = iota((peers, slots), 1)
        low = iota((peers, slots), 0) * slot_count
        at = place_rows(dot(ones_where((lane >= low) & (lane < low + slot_count)), used)[:, :1], slots)
        to_ref[...] = ones_where(iota((rows, slots), 0) == at)
        span = rows // SEGS
        at = jnp.where(at < 0, at, (at % span) * SEGS + at // span)
        steps_ref[...] = ones_where(iota((rows, slots), 0) == at)
        back_ref[...] = ones_where(iota((slots, rows), 1) == as_column(at))

    return pl.pallas_call(
        body,
        grid=(1,),
        in_specs=[pl.BlockSpec((slots, 128), lambda j: (0, 0))],
        out_specs=[whole((rows, slots)), whole((rows, slots)), whole((slots, rows))],
        out_shape=[
            jax.ShapeDtypeStruct((rows, slots), bf16),
            jax.ShapeDtypeStruct((rows, slots), bf16),
            jax.ShapeDtypeStruct((slots, rows), bf16),
        ],
        compiler_params=params(),
        cost_estimate=cost(1e6, 6 * rows * slots),
        name="place",
    )(received)


def unpack(received, to_rows, tile=512):
    slots, channels = received.shape
    rows = to_rows.shape[0]

    def body(hot_ref, in_ref, out_ref):
        out_ref[...] = dot(hot_ref[...], in_ref[...]).astype(bf16)

    return pl.pallas_call(
        body,
        grid=(channels // tile,),
        in_specs=[whole(to_rows.shape), cols((slots, tile))],
        out_specs=cols((rows, tile)),
        out_shape=jax.ShapeDtypeStruct((rows, channels), bf16),
        compiler_params=params(),
        cost_estimate=cost(2 * slots * rows * channels, 2 * (rows + slots) * channels),
        name="unpack",
    )(to_rows, received)


def finish(returned, planes, plane, back, tile=512):
    slots, channels = returned.shape
    _, rows, _ = planes.shape

    def body(back_ref, gate_ref, in_ref, out_ref):
        out_ref[...] = (gate_ref[0].astype(f32) * dot(back_ref[...], in_ref[...])).astype(bf16)

    return pl.pallas_call(
        body,
        grid=(channels // tile,),
        in_specs=[
            whole((rows, slots)),
            pl.BlockSpec((1, rows, tile), lambda j: (plane, 0, j)),
            cols((slots, tile)),
        ],
        out_specs=cols((rows, tile)),
        out_shape=jax.ShapeDtypeStruct((rows, channels), bf16),
        compiler_params=params(),
        cost_estimate=cost(2 * slots * rows * channels, 2 * (2 * rows + slots) * channels),
        name="finish",
    )(back, planes, returned)


def two_parts(table):
    high = table.astype(ml_dtypes.bfloat16)
    return high, (table - high.astype(np.float64)).astype(ml_dtypes.bfloat16)


def dft_tables(taps):
    points = 2 * taps
    k = np.arange(taps)[:, None].astype(np.float64)
    t = np.arange(points)[None, :].astype(np.float64)
    forward = np.concatenate(
        [np.cos(2 * np.pi * k * t / points), np.cos(np.pi * t), -np.sin(2 * np.pi * k[1:] * t / points)]
    )
    inverse = forward.T[taps:] * (2.0 / points)
    inverse[:, 0] *= 0.5
    inverse[:, taps] *= 0.5
    return np.concatenate(two_parts(forward)), np.concatenate(two_parts(inverse))


def side_by_side(rows):
    p = np.arange(rows)
    t = (p % SEGS) * (rows // SEGS) + p // SEGS
    return (t[:, None] == p[None, :]).astype(ml_dtypes.bfloat16)


def forward_dft(table, x):
    both = dot(table, x)
    half = both.shape[0] // 2
    return both[:half] + both[half:]


def inverse_dft(table, y):
    half = table.shape[0] // 2
    high = y.astype(bf16)
    low = (y - high.astype(f32)).astype(bf16)
    both = dot(table, high)
    return both[:half] + both[half:] + dot(table[:half], low)


def through_filter(spectrum, filter_ref, inverse_table):
    taps = spectrum.shape[0] // 2
    a, b = spectrum[:taps], spectrum[taps:]
    re, im, re_last = filter_ref[0], filter_ref[1], filter_ref[2]
    return inverse_dft(inverse_table, jnp.concatenate([a * re - b * im, a * im + b * re_last]))


def filter_spectrum(mr_filter, forward, tile=512):
    taps, channels = mr_filter.shape

    def body(taps_ref, fwd_ref, out_ref):
        fwd = fwd_ref[:, :taps]
        x = taps_ref[...]
        high = x.astype(bf16)
        low = (x - high.astype(f32)).astype(bf16)
        h = forward_dft(fwd, high) + dot(fwd[: 2 * taps], low)
        first = iota((taps, tile), 0) == 0
        out_ref[0] = h[:taps]
        out_ref[1] = jnp.where(first, 0.0, h[taps:])
        out_ref[2] = jnp.where(first, h[taps:], h[:taps])

    return pl.pallas_call(
        body,
        grid=(channels // tile,),
        in_specs=[cols((taps, tile)), whole(forward.shape)],
        out_specs=cols((3, taps, tile)),
        out_shape=jax.ShapeDtypeStruct((3, taps, channels), f32),
        compiler_params=params(),
        cost_estimate=cost(6 * 2 * taps * taps * channels, 16 * taps * channels),
        name="spectrum",
    )(mr_filter, forward)


def filter_rows(u, spectrum, forward, inverse, tile=512):
    rows, channels = u.shape
    taps = spectrum.shape[1]

    def body(u_ref, h_ref, fwd_ref, inv_ref, out_ref):
        for b in range(rows // taps):
            if b == 0:
                x = forward_dft(fwd_ref[:, taps:], u_ref[:taps])
            else:
                x = forward_dft(fwd_ref[...], u_ref[(b - 1) * taps : (b + 1) * taps])
            out_ref[b * taps : (b + 1) * taps] = through_filter(x, h_ref, inv_ref[...])

    return pl.pallas_call(
        body,
        grid=(channels // tile,),
        in_specs=[cols((rows, tile)), cols((3, taps, tile)), whole(forward.shape), whole(inverse.shape)],
        out_specs=cols((rows, tile)),
        out_shape=jax.ShapeDtypeStruct((rows, channels), f32),
        compiler_params=params(),
        cost_estimate=cost(14 * taps * rows * channels, 8 * rows * channels),
        name="taps",
    )(u, spectrum, forward, inverse)


def gate(received, to_rows, filtered, rim, spectrum, forward, inverse, beside, tile=512):
    slots, channels = received.shape
    rows = to_rows.shape[0]
    taps = spectrum.shape[1]

    def body(hot_ref, in_ref, filt_ref, rim_ref, h_ref, fwd_ref, inv_ref, beside_ref, out_ref):
        q = dot(hot_ref[...], in_ref[...])
        early = through_filter(forward_dft(fwd_ref[:, :taps], rim_ref[...]), h_ref, inv_ref[...])
        first = (q[:taps] * (filt_ref[:taps] + early)).astype(bf16)
        rest = (q[taps:] * filt_ref[taps:]).astype(bf16)
        out_ref[...] = dot(beside_ref[...], jnp.concatenate([first, rest])).astype(bf16)

    return pl.pallas_call(
        body,
        grid=(channels // tile,),
        in_specs=[
            whole(to_rows.shape),
            cols((slots, tile)),
            cols((rows, tile)),
            cols((taps, tile)),
            cols((3, taps, tile)),
            whole(forward.shape),
            whole(inverse.shape),
            whole((rows, rows)),
        ],
        out_specs=cols((rows, tile)),
        out_shape=jax.ShapeDtypeStruct((rows, channels), bf16),
        compiler_params=params(),
        cost_estimate=cost(2 * slots * rows * channels, (6 * rows + 2 * slots) * channels),
        name="gate",
    )(to_rows, received, filtered, rim, spectrum, forward, inverse, beside)


def project(tasks, blocks, own, other, weight, other_weight, tile=512):
    rows, depth = own.shape
    width = depth
    steps = width // tile
    adds = [add for _, _, _, add, _ in tasks if add is not None]
    shapes = [jax.ShapeDtypeStruct((take, width), kind) for _, _, splits, _, kind in tasks for take in splits]

    def body(blocks_ref, own_ref, other_ref, *rest):
        arrived = iter(rest[2 * len(tasks) : 2 * len(tasks) + len(adds)])
        outs = iter(rest[2 * len(tasks) + len(adds) :])
        for n, (_, low, splits, add, kind) in enumerate(tasks):
            at = slice(low, low + sum(splits))
            total = dot(own_ref[at], rest[2 * n][...]) + dot(other_ref[at], rest[2 * n + 1][...])
            if add is not None:
                total = total + next(arrived)[...].astype(f32)
            start = 0
            for take in splits:
                next(outs)[...] = total[start : start + take].astype(kind)
                start += take

    specs = [whole((rows, depth))] * 2
    operands = [own, other]
    for dx, *_ in tasks:
        spec = pl.BlockSpec(
            (depth, tile), functools.partial(lambda d, j, b: (0, b[d] * steps + j), dx)
        )
        specs += [spec, spec]
        operands += [weight, other_weight]
    for add in adds:
        specs.append(cols((add.shape[0], tile)))
        operands.append(add)
    total_rows = sum(shape.shape[0] for shape in shapes)
    return pl.pallas_call(
        body,
        grid_spec=pltpu.PrefetchScalarGridSpec(
            num_scalar_prefetch=1,
            grid=(steps,),
            in_specs=specs,
            out_specs=[cols((shape.shape[0], tile)) for shape in shapes],
        ),
        out_shape=shapes,
        compiler_params=params(),
        cost_estimate=cost(
            4 * depth * width * total_rows, 4 * depth * width * len(tasks) + 4 * rows * depth + 4 * total_rows * width
        ),
        name="project",
    )(blocks, *operands)


def rows_of(t):
    return pl.ds(pl.multiple_of(t * SEGS, SEGS), SEGS)


def spread(ref, which, lanes):
    return [jnp.broadcast_to(ref[which, n : n + 1, lanes], (SEGS, 128)) for n in range(ORDER)]


def total_of(terms):
    while len(terms) > 1:
        terms = [a + b for a, b in zip(terms[::2], terms[1::2])]
    return terms[0]


def end_states(table, own, arrived, k_li, last, coef, peers, tile=256):
    rows, width = own.shape
    half = rows // 2
    blocks = tile // 128

    def body(table_ref, own_ref, a0_ref, a1_ref, b0_ref, b1_ref, k_ref, last_ref, coef_ref, u_ref, seg_ref, end_ref):
        top = own_ref[:half].astype(f32) + a0_ref[...].astype(f32) + a1_ref[...].astype(f32)
        top = top * k_ref[:half].astype(f32)
        bottom = own_ref[half:].astype(f32) + b0_ref[...].astype(f32) + b1_ref[...].astype(f32)
        bottom = bottom * k_ref[half:].astype(f32)
        for cb in range(blocks):
            lanes = slice(cb * 128, (cb + 1) * 128)
            u_ref[cb, :half] = top[:, lanes]
            u_ref[cb, half:] = bottom[:, lanes]
        for cb in range(blocks):
            lanes = slice(cb * 128, (cb + 1) * 128)
            decay = spread(coef_ref, 0, lanes)

            def step(t, state):
                u = u_ref[cb, rows_of(t), :] * last_ref[rows_of(t), :]
                return tuple(d * s + u for d, s in zip(decay, state))

            state = lax.fori_loop(0, rows // SEGS, step, (jnp.zeros((SEGS, 128), f32),) * ORDER, unroll=8)
            for n in range(ORDER):
                seg_ref[cb, n * SEGS : (n + 1) * SEGS] = state[n]
            total = jnp.zeros((ORDER, 128), f32)
            for s in range(SEGS):
                keep = jnp.where(table_ref[s] == 0, coef_ref[1, :, lanes], 0.0)
                total = keep * total + seg_ref[cb, pl.ds(s, ORDER, stride=SEGS), :]
            for p in range(peers):
                end_ref[p * ORDER : (p + 1) * ORDER, lanes] = total.astype(bf16)

    return pl.pallas_call(
        body,
        grid_spec=pltpu.PrefetchScalarGridSpec(
            num_scalar_prefetch=1,
            grid=(width // tile,),
            in_specs=[
                cols((rows, tile)),
                cols((half, tile)),
                cols((half, tile)),
                cols((half, tile)),
                cols((half, tile)),
                cols((rows, tile)),
                whole(last.shape),
                cols((4, ORDER, tile)),
            ],
            out_specs=[
                leading((blocks, rows, 128)),
                leading((blocks, ORDER * SEGS, 128)),
                cols((peers * ORDER, tile)),
            ],
        ),
        out_shape=[
            jax.ShapeDtypeStruct((width // 128, rows, 128), f32),
            jax.ShapeDtypeStruct((width // 128, ORDER * SEGS, 128), f32),
            jax.ShapeDtypeStruct((peers * ORDER, width), bf16),
        ],
        compiler_params=params(),
        cost_estimate=cost(4e9, 12 * rows * width),
        name="ends",
    )(table, own, *arrived, k_li, last, coef)


def recur(table, segs, u, keep, coef, step_blocks=2):
    count, rows, _ = u.shape

    def body(table_ref, seg_ref, u_ref, keep_ref, coef_ref, li_ref, in_ref):
        for cb in range(step_blocks):
            lanes = slice(cb * 128, (cb + 1) * 128)
            enter = jnp.zeros((ORDER, 128), f32)
            for s in range(SEGS):
                in_ref[pl.ds(s, ORDER, stride=SEGS), :] = enter
                fade = jnp.where(table_ref[s] == 0, coef_ref[1, :, lanes], 0.0)
                enter = fade * enter + seg_ref[cb, pl.ds(s, ORDER, stride=SEGS), :]
            decay, weigh = spread(coef_ref, 0, lanes), spread(coef_ref, 3, lanes)

            def step(t, state):
                u, kept = u_ref[cb, rows_of(t), :], keep_ref[rows_of(t), :]
                state = tuple((d * s) * kept + u for d, s in zip(decay, state))
                li_ref[cb, rows_of(t), :] = total_of([w * s for w, s in zip(weigh, state)])
                return state

            state = tuple(in_ref[n * SEGS : (n + 1) * SEGS] for n in range(ORDER))
            lax.fori_loop(0, rows // SEGS, step, state, unroll=8)

    return pl.pallas_call(
        body,
        grid_spec=pltpu.PrefetchScalarGridSpec(
            num_scalar_prefetch=1,
            grid=(count // step_blocks,),
            in_specs=[
                leading((step_blocks, ORDER * SEGS, 128)),
                leading((step_blocks, rows, 128)),
                whole(keep.shape),
                cols((4, ORDER, step_blocks * 128)),
            ],
            out_specs=leading((step_blocks, rows, 128)),
            scratch_shapes=[pltpu.VMEM((ORDER * SEGS, 128), f32)],
        ),
        out_shape=jax.ShapeDtypeStruct(u.shape, f32),
        compiler_params=params(),
        cost_estimate=cost(8e9, 8 * count * rows * 128),
        name="recur",
    )(table, segs, u, keep, coef)


def carry_in(table, ends, li, unbroken, coef, back, peers, step_blocks=4):
    count, rows, _ = li.shape
    slots = back.shape[0]
    tile = step_blocks * 128

    def body(table_ref, ends_ref, li_ref, unbroken_ref, coef_ref, back_ref, out_ref, in_ref, sum_ref):
        def hop(j, carry):
            return jnp.where(table_ref[SEGS + j] == 0, coef_ref[2], 0.0) * carry + ends_ref[j].astype(f32)

        carry = lax.fori_loop(0, table_ref[SEGS + peers], hop, jnp.zeros((ORDER, tile), f32))
        for cb in range(step_blocks):
            lanes = slice(cb * 128, (cb + 1) * 128)
            enter = carry[:, lanes] * coef_ref[3, :, lanes]
            for s in range(SEGS):
                in_ref[pl.ds(s, ORDER, stride=SEGS), :] = enter
                enter = coef_ref[1, :, lanes] * enter
            decay = spread(coef_ref, 0, lanes)

            def step(t, state):
                state = tuple(d * s for d, s in zip(decay, state))
                more = total_of(list(state)) * unbroken_ref[rows_of(t), :]
                sum_ref[rows_of(t), lanes] = li_ref[cb, rows_of(t), :] + more
                return state

            state = tuple(in_ref[n * SEGS : (n + 1) * SEGS] for n in range(ORDER))
            lax.fori_loop(0, rows // SEGS, step, state, unroll=8)
        out_ref[...] = dot(back_ref[...], sum_ref[...].astype(bf16)).astype(bf16)

    return pl.pallas_call(
        body,
        grid_spec=pltpu.PrefetchScalarGridSpec(
            num_scalar_prefetch=1,
            grid=(count // step_blocks,),
            in_specs=[
                cols((peers, ORDER, tile)),
                leading((step_blocks, rows, 128)),
                whole(unbroken.shape),
                cols((4, ORDER, tile)),
                whole(back.shape),
            ],
            out_specs=cols((slots, tile)),
            scratch_shapes=[pltpu.VMEM((ORDER * SEGS, 128), f32), pltpu.VMEM((rows, tile), f32)],
        ),
        out_shape=jax.ShapeDtypeStruct((slots, count * 128), bf16),
        compiler_params=params(),
        cost_estimate=cost(4e9, 8 * count * rows * 128),
        name="carry",
    )(table, ends, li, unbroken, coef, back)


def along_x(shard, dx, dcore=0):
    count = lax.axis_size("tp") // 2
    pairs = [
        (2 * x + c, 2 * ((x + dx) % count) + (c + dcore) % 2) for x in range(count) for c in range(2)
    ]
    return lax.ppermute(shard, "tp", pairs)


def lane_mask(hit):
    return jnp.broadcast_to(jnp.where(hit, 0.0, 1.0).astype(f32)[:, None], (hit.shape[0], 128))


def swap(shard):
    return lax.all_to_all(shard, "ctx", split_axis=0, concat_axis=0, tiled=True)


def together(*arrays):
    return lax.optimization_barrier(arrays)


def on_device(projected, route, contig_len, mr_filter, out_weight, li_rate, li_residue):
    rows, _, channels = projected.shape
    peers = lax.axis_size("ctx")
    slot_count = 3 * rows // (2 * peers)
    taps = mr_filter.shape[0]
    half = rows // 2
    me = lax.axis_index("ctx").astype(i32)
    tp = lax.axis_index("tp").astype(i32)
    chip, core = tp // 2, tp % 2
    chips = lax.axis_size("tp") // 2
    planes = jnp.transpose(projected, (1, 0, 2))
    route_row = route.reshape(1, rows)
    me_row = me.reshape(1)
    span = rows // SEGS
    forward, inverse = (jnp.asarray(t) for t in dft_tables(taps))
    beside = jnp.asarray(side_by_side(rows))

    packed_kv = pack_product(planes, route_row, 1, 2, slot_count, peers)
    packed_kv, other_source = together(packed_kv, out_weight)
    other_weight = along_x(other_source, 0, 1)
    got_kv = swap(packed_kv)
    packed_q, packed_k, to_loader = pack_two(planes, route_row, 0, 4, slot_count, peers)

    order = jnp.arange(contig_len.shape[0], dtype=i32)
    starts = jnp.sum(jnp.where(order[:, None] < order[None, :], contig_len[:, None], 0), axis=0)
    here = me * rows + jnp.arange(SEGS, dtype=i32)[None, :] * span + jnp.arange(span, dtype=i32)[:, None]
    here = here.reshape(rows, 1)
    seg_last = here - here % span + (span - 1)
    seen, behind = starts[None, :] <= here, starts[None, :] > here
    keep = lane_mask(jnp.any(starts[None, :] == here, axis=1))
    last = lane_mask(jnp.any(behind & (starts[None, :] <= seg_last), axis=1))
    unbroken = lane_mask(jnp.any(seen & (starts[None, :] >= me * rows), axis=1))
    seg_ids = me * SEGS + jnp.arange(SEGS, dtype=i32)
    seg_has = jnp.any(seg_ids[:, None] == (starts // span)[None, :], axis=1)
    dev_has = jnp.any(jnp.arange(peers, dtype=i32)[:, None] == (starts // rows)[None, :], axis=1)
    table = jnp.concatenate([seg_has.astype(i32), dev_has.astype(i32), me_row])
    mode_weight = li_residue * jnp.sqrt(-jnp.expm1(-2.0 * li_rate))
    coef = jnp.stack([jnp.exp(-li_rate), jnp.exp(-li_rate * span), jnp.exp(-li_rate * rows), mode_weight])
    spectrum = filter_spectrum(mr_filter, forward)

    blocks = jnp.stack([2 * ((chip + d) % chips) + core for d in range(chips)]).astype(i32)

    got_kv, packed_q, coef, spectrum = together(got_kv, packed_q, coef, spectrum)
    got_q = swap(packed_q)
    to_rows, to_steps, to_slots = place_matrices(got_kv, rows, slot_count, peers)
    u_mr = unpack(got_kv, to_rows)
    rim = lax.ppermute(u_mr[rows - taps :], "ctx", [(i, i + 1) for i in range(peers - 1)])
    filtered = filter_rows(u_mr, spectrum, forward, inverse)
    got_q, filtered, packed_k = together(got_q, filtered, packed_k)
    got_k = swap(packed_k)
    gated = gate(got_q, to_rows, filtered, rim, spectrum, forward, inverse, beside)
    other = along_x(gated, 0, 1)
    mm = functools.partial(project, own=gated, weight=out_weight, other_weight=other_weight)
    far_a, far_b = mm([(2, 0, (half, half), None, bf16)], blocks, other=other)
    blocks, far_a, far_b = together(blocks, far_a, far_b)
    pass_a, pass_b = along_x(far_a, 1), along_x(far_b, -1)
    up_b, down_a = mm([(1, half, (half,), None, bf16), (3, 0, (half,), None, bf16)], blocks, other=other)
    up_b, down_a, blocks = together(up_b, down_a, blocks)
    from_low_b, from_high_a = along_x(up_b, 1), along_x(down_a, -1)
    up_a, down_b = mm([(1, 0, (half,), pass_a, bf16), (3, half, (half,), pass_b, bf16)], blocks, other=other)
    up_a, down_b, blocks, got_k = together(up_a, down_b, blocks, got_k)
    from_low_a, from_high_b = along_x(up_a, 1), along_x(down_b, -1)
    [mine] = mm([(0, 0, (rows,), None, bf16)], blocks, other=other)
    k_li = unpack(got_k, to_steps)
    u, segs, end = end_states(
        table, mine, [from_low_a, from_high_a, from_low_b, from_high_b], k_li, last, coef, peers
    )
    ends = swap(end).reshape(peers, ORDER, channels)
    li = recur(table, segs, u, keep, coef)
    returned = swap(carry_in(table, ends, li, unbroken, coef, to_slots, peers))
    return finish(returned, planes, 3, to_loader)


def solution(mesh):
    return jax.shard_map(
        on_device,
        mesh=mesh,
        in_specs=(
            P("ctx", None, "tp"),
            P("ctx"),
            P(),
            P(None, "tp"),
            P("tp", None),
            P(None, "tp"),
            P(None, "tp"),
        ),
        out_specs=P("ctx", "tp"),
        check_vma=False,
    )
```

```python
import functools

import jax
import jax.numpy as jnp
import ml_dtypes
import numpy as np
from jax import lax
from jax.experimental import pallas as pl
from jax.experimental.pallas import tpu as pltpu
from jax.sharding import PartitionSpec as P

f32 = jnp.float32
bf16 = jnp.bfloat16
i32 = jnp.int32
SEGS = 8
ORDER = 16
EMPTY = 64.0
MIB = 48


def dot(a, b):
    return jnp.dot(a, b, preferred_element_type=f32)


def iota(shape, dim):
    return lax.broadcasted_iota(i32, shape, dim)


def ones_where(mask):
    return jnp.where(mask, 1.0, 0.0).astype(bf16)


def params(mib=MIB):
    return pltpu.CompilerParams(vmem_limit_bytes=mib * 2**20)


def cost(flops, nbytes):
    return pl.CostEstimate(flops=int(flops) // 10, bytes_accessed=int(nbytes) // 10, transcendentals=0)


def in_hbm(x):
    return pltpu.with_memory_space_constraint(x, pltpu.HBM)


def whole(shape):
    return pl.BlockSpec(shape, lambda *_: (0,) * len(shape))


def cols(shape):
    return pl.BlockSpec(shape, lambda j, *_: (0,) * (len(shape) - 1) + (j,))


def leading(shape):
    return pl.BlockSpec(shape, lambda j, *_: (j,) + (0,) * (len(shape) - 1))


def as_column(row):
    return jnp.transpose(jnp.broadcast_to(row.astype(f32), (128, row.shape[1])))[:, :1].astype(i32)


def send_slots(route, peers, slot_count):
    rows = route.shape[1]
    hot = iota((peers, rows), 0) == route
    earlier = ones_where(iota((rows, rows), 0) < iota((rows, rows), 1))
    rank = dot(ones_where(hot), earlier)
    rank = jnp.sum(jnp.where(hot, rank, 0.0), axis=0, keepdims=True)
    return route * slot_count + rank.astype(i32)


def place_rows(count, slots):
    peers = count.shape[0]
    per = slots // peers
    lane = iota((peers, slots), 1)
    low = iota((peers, slots), 0) * per
    mine = (lane >= low) & (lane < low + per)
    before = jnp.sum(jnp.where(lane >= low + per, count, 0.0), axis=0, keepdims=True)
    held = jnp.sum(jnp.where(mine, count, 0.0), axis=0, keepdims=True)
    within = jnp.sum(jnp.where(mine, (lane - low).astype(f32), 0.0), axis=0, keepdims=True)
    return jnp.where(within < held, before + within, -1.0).astype(i32)


def pack_product(planes, route, first, second, slot_count, peers, tile=512):
    _, rows, channels = planes.shape
    slots = peers * slot_count

    def body(route_ref, a_ref, b_ref, out_ref, hot_ref, fill_ref):
        @pl.when(pl.program_id(0) == 0)
        def _():
            hot = ones_where(iota((slots, rows), 0) == send_slots(route_ref[...], peers, slot_count))
            hot_ref[...] = hot
            fill_ref[...] = EMPTY * (1.0 - dot(hot, jnp.ones((rows, 128), bf16)))

        x = (a_ref[0].astype(f32) * b_ref[0].astype(f32)).astype(bf16)
        out_ref[...] = (dot(hot_ref[...], x) + fill_ref[:, :1]).astype(bf16)

    return pl.pallas_call(
        body,
        grid=(channels // tile,),
        in_specs=[whole((1, rows))]
        + [pl.BlockSpec((1, rows, tile), functools.partial(lambda s, j: (s, 0, j), s)) for s in (first, second)],
        out_specs=cols((slots, tile)),
        out_shape=jax.ShapeDtypeStruct((slots, channels), bf16),
        scratch_shapes=[pltpu.VMEM((slots, rows), bf16), pltpu.VMEM((slots, 128), f32)],
        compiler_params=params(),
        cost_estimate=cost(2 * slots * rows * channels, 2 * (2 * rows + slots) * channels),
        name="pack_kv",
    )(in_hbm(route), planes, planes)


def pack_two(planes, route, first, second, slot_count, peers, tile=512):
    _, rows, channels = planes.shape
    slots = peers * slot_count

    def body(route_ref, a_ref, b_ref, out_a_ref, out_b_ref, back_ref, hot_ref):
        @pl.when(pl.program_id(0) == 0)
        def _():
            slot = send_slots(route_ref[...], peers, slot_count)
            hot_ref[...] = ones_where(iota((slots, rows), 0) == slot)
            back_ref[...] = ones_where(iota((rows, slots), 1) == as_column(slot))

        out_a_ref[...] = dot(hot_ref[...], a_ref[0]).astype(bf16)
        out_b_ref[...] = dot(hot_ref[...], b_ref[0]).astype(bf16)

    return pl.pallas_call(
        body,
        grid=(channels // tile,),
        in_specs=[whole((1, rows))]
        + [pl.BlockSpec((1, rows, tile), functools.partial(lambda s, j: (s, 0, j), s)) for s in (first, second)],
        out_specs=[cols((slots, tile)), cols((slots, tile)), whole((rows, slots))],
        out_shape=[
            jax.ShapeDtypeStruct((slots, channels), bf16),
            jax.ShapeDtypeStruct((slots, channels), bf16),
            jax.ShapeDtypeStruct((rows, slots), bf16),
        ],
        scratch_shapes=[pltpu.VMEM((slots, rows), bf16)],
        compiler_params=params(),
        cost_estimate=cost(4 * slots * rows * channels, 4 * (rows + slots) * channels),
        name="pack_two",
    )(in_hbm(route), planes, planes)


def place_matrices(received, rows, slot_count, peers):
    slots = received.shape[0]

    def body(in_ref, to_ref, steps_ref, back_ref):
        used = ones_where(in_ref[...].astype(f32) < 0.75 * EMPTY)
        lane = iota((peers, slots), 1)
        low = iota((peers, slots), 0) * slot_count
        at = place_rows(dot(ones_where((lane >= low) & (lane < low + slot_count)), used)[:, :1], slots)
        to_ref[...] = ones_where(iota((rows, slots), 0) == at)
        span = rows // SEGS
        at = jnp.where(at < 0, at, (at % span) * SEGS + at // span)
        steps_ref[...] = ones_where(iota((rows, slots), 0) == at)
        back_ref[...] = ones_where(iota((slots, rows), 1) == as_column(at))

    return pl.pallas_call(
        body,
        grid=(1,),
        in_specs=[pl.BlockSpec((slots, 128), lambda j: (0, 0))],
        out_specs=[whole((rows, slots)), whole((rows, slots)), whole((slots, rows))],
        out_shape=[
            jax.ShapeDtypeStruct((rows, slots), bf16),
            jax.ShapeDtypeStruct((rows, slots), bf16),
            jax.ShapeDtypeStruct((slots, rows), bf16),
        ],
        compiler_params=params(),
        cost_estimate=cost(1e6, 6 * rows * slots),
        name="place",
    )(received)


def unpack(received, to_rows, tile=512):
    slots, channels = received.shape
    rows = to_rows.shape[0]

    def body(hot_ref, in_ref, out_ref):
        out_ref[...] = dot(hot_ref[...], in_ref[...]).astype(bf16)

    return pl.pallas_call(
        body,
        grid=(channels // tile,),
        in_specs=[whole(to_rows.shape), cols((slots, tile))],
        out_specs=cols((rows, tile)),
        out_shape=jax.ShapeDtypeStruct((rows, channels), bf16),
        compiler_params=params(),
        cost_estimate=cost(2 * slots * rows * channels, 2 * (rows + slots) * channels),
        name="unpack",
    )(to_rows, received)


def finish(returned, planes, plane, back, tile=512):
    slots, channels = returned.shape
    _, rows, _ = planes.shape

    def body(back_ref, gate_ref, in_ref, out_ref):
        out_ref[...] = (gate_ref[0].astype(f32) * dot(back_ref[...], in_ref[...])).astype(bf16)

    return pl.pallas_call(
        body,
        grid=(channels // tile,),
        in_specs=[
            whole((rows, slots)),
            pl.BlockSpec((1, rows, tile), lambda j: (plane, 0, j)),
            cols((slots, tile)),
        ],
        out_specs=cols((rows, tile)),
        out_shape=jax.ShapeDtypeStruct((rows, channels), bf16),
        compiler_params=params(),
        cost_estimate=cost(2 * slots * rows * channels, 2 * (2 * rows + slots) * channels),
        name="finish",
    )(back, planes, returned)


def two_parts(table):
    high = table.astype(ml_dtypes.bfloat16)
    return high, (table - high.astype(np.float64)).astype(ml_dtypes.bfloat16)


def dft_tables(taps):
    points = 2 * taps
    k = np.arange(taps)[:, None].astype(np.float64)
    t = np.arange(points)[None, :].astype(np.float64)
    forward = np.concatenate(
        [np.cos(2 * np.pi * k * t / points), np.cos(np.pi * t), -np.sin(2 * np.pi * k[1:] * t / points)]
    )
    inverse = forward.T[taps:] * (2.0 / points)
    inverse[:, 0] *= 0.5
    inverse[:, taps] *= 0.5
    return np.concatenate(two_parts(forward)), np.concatenate(two_parts(inverse))


def side_by_side(rows):
    p = np.arange(rows)
    t = (p % SEGS) * (rows // SEGS) + p // SEGS
    return (t[:, None] == p[None, :]).astype(ml_dtypes.bfloat16)


def forward_dft(table, x):
    both = dot(table, x)
    half = both.shape[0] // 2
    return both[:half] + both[half:]


def inverse_dft(table, y):
    half = table.shape[0] // 2
    high = y.astype(bf16)
    low = (y - high.astype(f32)).astype(bf16)
    both = dot(table, high)
    return both[:half] + both[half:] + dot(table[:half], low)


def through_filter(spectrum, filter_ref, inverse_table):
    taps = spectrum.shape[0] // 2
    a, b = spectrum[:taps], spectrum[taps:]
    re, im, re_last = filter_ref[0], filter_ref[1], filter_ref[2]
    return inverse_dft(inverse_table, jnp.concatenate([a * re - b * im, a * im + b * re_last]))


def filter_spectrum(mr_filter, forward, tile=512):
    taps, channels = mr_filter.shape

    def body(taps_ref, fwd_ref, out_ref):
        fwd = fwd_ref[:, :taps]
        x = taps_ref[...]
        high = x.astype(bf16)
        low = (x - high.astype(f32)).astype(bf16)
        h = forward_dft(fwd, high) + dot(fwd[: 2 * taps], low)
        first = iota((taps, tile), 0) == 0
        out_ref[0] = h[:taps]
        out_ref[1] = jnp.where(first, 0.0, h[taps:])
        out_ref[2] = jnp.where(first, h[taps:], h[:taps])

    return pl.pallas_call(
        body,
        grid=(channels // tile,),
        in_specs=[cols((taps, tile)), whole(forward.shape)],
        out_specs=cols((3, taps, tile)),
        out_shape=jax.ShapeDtypeStruct((3, taps, channels), f32),
        compiler_params=params(),
        cost_estimate=cost(6 * 2 * taps * taps * channels, 16 * taps * channels),
        name="spectrum",
    )(mr_filter, forward)


def filter_rows(u, spectrum, forward, inverse, tile=512):
    rows, channels = u.shape
    taps = spectrum.shape[1]

    def body(u_ref, h_ref, fwd_ref, inv_ref, out_ref):
        for b in range(rows // taps):
            if b == 0:
                x = forward_dft(fwd_ref[:, taps:], u_ref[:taps])
            else:
                x = forward_dft(fwd_ref[...], u_ref[(b - 1) * taps : (b + 1) * taps])
            out_ref[b * taps : (b + 1) * taps] = through_filter(x, h_ref, inv_ref[...])

    return pl.pallas_call(
        body,
        grid=(channels // tile,),
        in_specs=[cols((rows, tile)), cols((3, taps, tile)), whole(forward.shape), whole(inverse.shape)],
        out_specs=cols((rows, tile)),
        out_shape=jax.ShapeDtypeStruct((rows, channels), f32),
        compiler_params=params(),
        cost_estimate=cost(14 * taps * rows * channels, 8 * rows * channels),
        name="taps",
    )(u, spectrum, forward, inverse)


def gate(received, to_rows, filtered, rim, spectrum, forward, inverse, beside, tile=512):
    slots, channels = received.shape
    rows = to_rows.shape[0]
    taps = spectrum.shape[1]

    def body(hot_ref, in_ref, filt_ref, rim_ref, h_ref, fwd_ref, inv_ref, beside_ref, out_ref):
        q = dot(hot_ref[...], in_ref[...])
        early = through_filter(forward_dft(fwd_ref[:, :taps], rim_ref[...]), h_ref, inv_ref[...])
        first = (q[:taps] * (filt_ref[:taps] + early)).astype(bf16)
        rest = (q[taps:] * filt_ref[taps:]).astype(bf16)
        out_ref[...] = dot(beside_ref[...], jnp.concatenate([first, rest])).astype(bf16)

    return pl.pallas_call(
        body,
        grid=(channels // tile,),
        in_specs=[
            whole(to_rows.shape),
            cols((slots, tile)),
            cols((rows, tile)),
            cols((taps, tile)),
            cols((3, taps, tile)),
            whole(forward.shape),
            whole(inverse.shape),
            whole((rows, rows)),
        ],
        out_specs=cols((rows, tile)),
        out_shape=jax.ShapeDtypeStruct((rows, channels), bf16),
        compiler_params=params(),
        cost_estimate=cost(2 * slots * rows * channels, (6 * rows + 2 * slots) * channels),
        name="gate",
    )(in_hbm(to_rows), in_hbm(received), filtered, rim, spectrum, forward, inverse, in_hbm(beside))


def project(tasks, blocks, own, other, weight, other_weight, tile=512):
    rows, depth = own.shape
    width = depth
    steps = width // tile
    adds = [add for _, _, _, add, _ in tasks if add is not None]
    shapes = [jax.ShapeDtypeStruct((take, width), kind) for _, _, splits, _, kind in tasks for take in splits]

    def body(blocks_ref, own_ref, other_ref, *rest):
        arrived = iter(rest[2 * len(tasks) : 2 * len(tasks) + len(adds)])
        outs = iter(rest[2 * len(tasks) + len(adds) :])
        for n, (_, low, splits, add, kind) in enumerate(tasks):
            at = slice(low, low + sum(splits))
            total = dot(own_ref[at], rest[2 * n][...]) + dot(other_ref[at], rest[2 * n + 1][...])
            if add is not None:
                total = total + next(arrived)[...].astype(f32)
            start = 0
            for take in splits:
                next(outs)[...] = total[start : start + take].astype(kind)
                start += take

    specs = [whole((rows, depth))] * 2
    operands = [own, other]
    for dx, *_ in tasks:
        spec = pl.BlockSpec(
            (depth, tile), functools.partial(lambda d, j, b: (0, b[d] * steps + j), dx)
        )
        specs += [spec, spec]
        operands += [weight, other_weight]
    for add in adds:
        specs.append(cols((add.shape[0], tile)))
        operands.append(add)
    total_rows = sum(shape.shape[0] for shape in shapes)
    return pl.pallas_call(
        body,
        grid_spec=pltpu.PrefetchScalarGridSpec(
            num_scalar_prefetch=1,
            grid=(steps,),
            in_specs=specs,
            out_specs=[cols((shape.shape[0], tile)) for shape in shapes],
        ),
        out_shape=shapes,
        compiler_params=params(),
        cost_estimate=cost(
            4 * depth * width * total_rows, 4 * depth * width * len(tasks) + 4 * rows * depth + 4 * total_rows * width
        ),
        name="project",
    )(blocks, *operands)


def rows_of(t):
    return pl.ds(pl.multiple_of(t * SEGS, SEGS), SEGS)


def spread(ref, which, lanes):
    return [jnp.broadcast_to(ref[which, n : n + 1, lanes], (SEGS, 128)) for n in range(ORDER)]


def total_of(terms):
    while len(terms) > 1:
        terms = [a + b for a, b in zip(terms[::2], terms[1::2])]
    return terms[0]


def end_states(table, own, arrived, k_li, last, coef, peers, tile=256):
    rows, width = own.shape
    half = rows // 2
    blocks = tile // 128

    def body(table_ref, own_ref, a0_ref, a1_ref, b0_ref, b1_ref, k_ref, last_ref, coef_ref, u_ref, seg_ref, end_ref):
        top = own_ref[:half].astype(f32) + a0_ref[...].astype(f32) + a1_ref[...].astype(f32)
        top = top * k_ref[:half].astype(f32)
        bottom = own_ref[half:].astype(f32) + b0_ref[...].astype(f32) + b1_ref[...].astype(f32)
        bottom = bottom * k_ref[half:].astype(f32)
        for cb in range(blocks):
            lanes = slice(cb * 128, (cb + 1) * 128)
            u_ref[cb, :half] = top[:, lanes]
            u_ref[cb, half:] = bottom[:, lanes]
        for cb in range(blocks):
            lanes = slice(cb * 128, (cb + 1) * 128)
            decay = spread(coef_ref, 0, lanes)

            def step(t, state):
                u = u_ref[cb, rows_of(t), :] * last_ref[rows_of(t), :]
                return tuple(d * s + u for d, s in zip(decay, state))

            state = lax.fori_loop(0, rows // SEGS, step, (jnp.zeros((SEGS, 128), f32),) * ORDER, unroll=8)
            for n in range(ORDER):
                seg_ref[cb, n * SEGS : (n + 1) * SEGS] = state[n]
            total = jnp.zeros((ORDER, 128), f32)
            for s in range(SEGS):
                keep = jnp.where(table_ref[s] == 0, coef_ref[1, :, lanes], 0.0)
                total = keep * total + seg_ref[cb, pl.ds(s, ORDER, stride=SEGS), :]
            for p in range(peers):
                end_ref[p * ORDER : (p + 1) * ORDER, lanes] = total.astype(bf16)

    return pl.pallas_call(
        body,
        grid_spec=pltpu.PrefetchScalarGridSpec(
            num_scalar_prefetch=1,
            grid=(width // tile,),
            in_specs=[
                cols((rows, tile)),
                cols((half, tile)),
                cols((half, tile)),
                cols((half, tile)),
                cols((half, tile)),
                cols((rows, tile)),
                whole(last.shape),
                cols((4, ORDER, tile)),
            ],
            out_specs=[
                leading((blocks, rows, 128)),
                leading((blocks, ORDER * SEGS, 128)),
                cols((peers * ORDER, tile)),
            ],
        ),
        out_shape=[
            jax.ShapeDtypeStruct((width // 128, rows, 128), f32),
            jax.ShapeDtypeStruct((width // 128, ORDER * SEGS, 128), f32),
            jax.ShapeDtypeStruct((peers * ORDER, width), bf16),
        ],
        compiler_params=params(),
        cost_estimate=cost(4e9, 12 * rows * width),
        name="ends",
    )(table, own, *arrived, k_li, last, coef)


def recur(table, segs, u, keep, coef, step_blocks=2):
    count, rows, _ = u.shape

    def body(table_ref, seg_ref, u_ref, keep_ref, coef_ref, li_ref, in_ref):
        for cb in range(step_blocks):
            lanes = slice(cb * 128, (cb + 1) * 128)
            enter = jnp.zeros((ORDER, 128), f32)
            for s in range(SEGS):
                in_ref[pl.ds(s, ORDER, stride=SEGS), :] = enter
                fade = jnp.where(table_ref[s] == 0, coef_ref[1, :, lanes], 0.0)
                enter = fade * enter + seg_ref[cb, pl.ds(s, ORDER, stride=SEGS), :]
            decay, weigh = spread(coef_ref, 0, lanes), spread(coef_ref, 3, lanes)

            def step(t, state):
                u, kept = u_ref[cb, rows_of(t), :], keep_ref[rows_of(t), :]
                state = tuple((d * s) * kept + u for d, s in zip(decay, state))
                li_ref[cb, rows_of(t), :] = total_of([w * s for w, s in zip(weigh, state)])
                return state

            state = tuple(in_ref[n * SEGS : (n + 1) * SEGS] for n in range(ORDER))
            lax.fori_loop(0, rows // SEGS, step, state, unroll=8)

    return pl.pallas_call(
        body,
        grid_spec=pltpu.PrefetchScalarGridSpec(
            num_scalar_prefetch=1,
            grid=(count // step_blocks,),
            in_specs=[
                leading((step_blocks, ORDER * SEGS, 128)),
                leading((step_blocks, rows, 128)),
                whole(keep.shape),
                cols((4, ORDER, step_blocks * 128)),
            ],
            out_specs=leading((step_blocks, rows, 128)),
            scratch_shapes=[pltpu.VMEM((ORDER * SEGS, 128), f32)],
        ),
        out_shape=jax.ShapeDtypeStruct(u.shape, f32),
        compiler_params=params(),
        cost_estimate=cost(8e9, 8 * count * rows * 128),
        name="recur",
    )(table, segs, in_hbm(u), keep, coef)


def carry_in(table, ends, li, unbroken, coef, back, peers, step_blocks=4):
    count, rows, _ = li.shape
    slots = back.shape[0]
    tile = step_blocks * 128

    def body(table_ref, ends_ref, li_ref, unbroken_ref, coef_ref, back_ref, out_ref, in_ref, sum_ref):
        def hop(j, carry):
            return jnp.where(table_ref[SEGS + j] == 0, coef_ref[2], 0.0) * carry + ends_ref[j].astype(f32)

        carry = lax.fori_loop(0, table_ref[SEGS + peers], hop, jnp.zeros((ORDER, tile), f32))
        for cb in range(step_blocks):
            lanes = slice(cb * 128, (cb + 1) * 128)
            enter = carry[:, lanes] * coef_ref[3, :, lanes]
            for s in range(SEGS):
                in_ref[pl.ds(s, ORDER, stride=SEGS), :] = enter
                enter = coef_ref[1, :, lanes] * enter
            decay = spread(coef_ref, 0, lanes)

            def step(t, state):
                state = tuple(d * s for d, s in zip(decay, state))
                more = total_of(list(state)) * unbroken_ref[rows_of(t), :]
                sum_ref[rows_of(t), lanes] = li_ref[cb, rows_of(t), :] + more
                return state

            state = tuple(in_ref[n * SEGS : (n + 1) * SEGS] for n in range(ORDER))
            lax.fori_loop(0, rows // SEGS, step, state, unroll=8)
        out_ref[...] = dot(back_ref[...], sum_ref[...].astype(bf16)).astype(bf16)

    return pl.pallas_call(
        body,
        grid_spec=pltpu.PrefetchScalarGridSpec(
            num_scalar_prefetch=1,
            grid=(count // step_blocks,),
            in_specs=[
                cols((peers, ORDER, tile)),
                leading((step_blocks, rows, 128)),
                whole(unbroken.shape),
                cols((4, ORDER, tile)),
                whole(back.shape),
            ],
            out_specs=cols((slots, tile)),
            scratch_shapes=[pltpu.VMEM((ORDER * SEGS, 128), f32), pltpu.VMEM((rows, tile), f32)],
        ),
        out_shape=jax.ShapeDtypeStruct((slots, count * 128), bf16),
        compiler_params=params(),
        cost_estimate=cost(4e9, 8 * count * rows * 128),
        name="carry",
    )(table, ends, li, unbroken, coef, in_hbm(back))


def along_x(shard, dx, dcore=0):
    count = lax.axis_size("tp") // 2
    pairs = [
        (2 * x + c, 2 * ((x + dx) % count) + (c + dcore) % 2) for x in range(count) for c in range(2)
    ]
    return lax.ppermute(shard, "tp", pairs)


def lane_mask(hit):
    return jnp.broadcast_to(jnp.where(hit, 0.0, 1.0).astype(f32)[:, None], (hit.shape[0], 128))


def swap(shard):
    return lax.all_to_all(shard, "ctx", split_axis=0, concat_axis=0, tiled=True)


def together(*arrays):
    return lax.optimization_barrier(arrays)


def on_device(projected, route, contig_len, mr_filter, out_weight, li_rate, li_residue):
    rows, _, channels = projected.shape
    peers = lax.axis_size("ctx")
    slot_count = 3 * rows // (2 * peers)
    taps = mr_filter.shape[0]
    half = rows // 2
    me = lax.axis_index("ctx").astype(i32)
    tp = lax.axis_index("tp").astype(i32)
    chip, core = tp // 2, tp % 2
    chips = lax.axis_size("tp") // 2
    planes = jnp.transpose(projected, (1, 0, 2))
    route_row = route.reshape(1, rows)
    me_row = me.reshape(1)
    span = rows // SEGS
    forward, inverse = (jnp.asarray(t) for t in dft_tables(taps))
    beside = jnp.asarray(side_by_side(rows))

    packed_kv = pack_product(planes, route_row, 1, 2, slot_count, peers)
    packed_kv, other_source = together(packed_kv, out_weight)
    other_weight = along_x(other_source, 0, 1)
    got_kv = swap(packed_kv)
    packed_q, packed_k, to_loader = pack_two(planes, route_row, 0, 4, slot_count, peers)

    order = jnp.arange(contig_len.shape[0], dtype=i32)
    starts = jnp.sum(jnp.where(order[:, None] < order[None, :], contig_len[:, None], 0), axis=0)
    here = me * rows + jnp.arange(SEGS, dtype=i32)[None, :] * span + jnp.arange(span, dtype=i32)[:, None]
    here = here.reshape(rows, 1)
    seg_last = here - here % span + (span - 1)
    seen, behind = starts[None, :] <= here, starts[None, :] > here
    keep = lane_mask(jnp.any(starts[None, :] == here, axis=1))
    last = lane_mask(jnp.any(behind & (starts[None, :] <= seg_last), axis=1))
    unbroken = lane_mask(jnp.any(seen & (starts[None, :] >= me * rows), axis=1))
    seg_ids = me * SEGS + jnp.arange(SEGS, dtype=i32)
    seg_has = jnp.any(seg_ids[:, None] == (starts // span)[None, :], axis=1)
    dev_has = jnp.any(jnp.arange(peers, dtype=i32)[:, None] == (starts // rows)[None, :], axis=1)
    table = jnp.concatenate([seg_has.astype(i32), dev_has.astype(i32), me_row])
    mode_weight = li_residue * jnp.sqrt(-jnp.expm1(-2.0 * li_rate))
    coef = jnp.stack([jnp.exp(-li_rate), jnp.exp(-li_rate * span), jnp.exp(-li_rate * rows), mode_weight])
    spectrum = filter_spectrum(mr_filter, forward)

    blocks = jnp.stack([2 * ((chip + d) % chips) + core for d in range(chips)]).astype(i32)

    got_kv, packed_q, coef, spectrum = together(got_kv, packed_q, coef, spectrum)
    got_q = swap(packed_q)
    to_rows, to_steps, to_slots = place_matrices(got_kv, rows, slot_count, peers)
    u_mr = unpack(got_kv, to_rows)
    rim = lax.ppermute(u_mr[rows - taps :], "ctx", [(i, i + 1) for i in range(peers - 1)])
    filtered = filter_rows(u_mr, spectrum, forward, inverse)
    got_q, filtered, packed_k = together(got_q, filtered, packed_k)
    got_k = swap(packed_k)
    gated = gate(got_q, to_rows, filtered, rim, spectrum, forward, inverse, beside)
    other = along_x(gated, 0, 1)
    mm = functools.partial(project, own=gated, weight=out_weight, other_weight=other_weight)
    far_a, far_b = mm([(2, 0, (half, half), None, bf16)], blocks, other=other)
    blocks, far_a, far_b = together(blocks, far_a, far_b)
    pass_a, pass_b = along_x(far_a, 1), along_x(far_b, -1)
    up_b, down_a = mm([(1, half, (half,), None, bf16), (3, 0, (half,), None, bf16)], blocks, other=other)
    up_b, down_a, blocks = together(up_b, down_a, blocks)
    from_low_b, from_high_a = along_x(up_b, 1), along_x(down_a, -1)
    up_a, down_b = mm([(1, 0, (half,), pass_a, bf16), (3, half, (half,), pass_b, bf16)], blocks, other=other)
    up_a, down_b, blocks, got_k = together(up_a, down_b, blocks, got_k)
    from_low_a, from_high_b = along_x(up_a, 1), along_x(down_b, -1)
    [mine] = mm([(0, 0, (rows,), None, bf16)], blocks, other=other)
    k_li = unpack(got_k, to_steps)
    u, segs, end = end_states(
        table, mine, [from_low_a, from_high_a, from_low_b, from_high_b], k_li, last, coef, peers
    )
    ends = swap(end).reshape(peers, ORDER, channels)
    li = recur(table, segs, u, keep, coef)
    returned = swap(carry_in(table, ends, li, unbroken, coef, to_slots, peers))
    return finish(returned, planes, 3, to_loader)


def solution(mesh):
    return jax.shard_map(
        on_device,
        mesh=mesh,
        in_specs=(
            P("ctx", None, "tp"),
            P("ctx"),
            P(),
            P(None, "tp"),
            P("tp", None),
            P(None, "tp"),
            P(None, "tp"),
        ),
        out_specs=P("ctx", "tp"),
        check_vma=False,
    )
```

```python
import functools

import jax
import jax.numpy as jnp
import ml_dtypes
import numpy as np
from jax import lax
from jax.experimental import pallas as pl
from jax.experimental.pallas import tpu as pltpu
from jax.sharding import PartitionSpec as P

f32 = jnp.float32
bf16 = jnp.bfloat16
i32 = jnp.int32
SEGS = 8
ORDER = 16
EMPTY = 64.0
MIB = 48


def dot(a, b):
    return jnp.dot(a, b, preferred_element_type=f32)


def iota(shape, dim):
    return lax.broadcasted_iota(i32, shape, dim)


def ones_where(mask):
    return jnp.where(mask, 1.0, 0.0).astype(bf16)


def params(mib=MIB):
    return pltpu.CompilerParams(vmem_limit_bytes=mib * 2**20)


def cost(flops, nbytes):
    return pl.CostEstimate(flops=int(flops) // 10, bytes_accessed=int(nbytes) // 10, transcendentals=0)


def in_hbm(x):
    return pltpu.with_memory_space_constraint(x, pltpu.HBM)


def whole(shape):
    return pl.BlockSpec(shape, lambda *_: (0,) * len(shape))


def cols(shape):
    return pl.BlockSpec(shape, lambda j, *_: (0,) * (len(shape) - 1) + (j,))


def leading(shape):
    return pl.BlockSpec(shape, lambda j, *_: (j,) + (0,) * (len(shape) - 1))


def as_column(row):
    return jnp.transpose(jnp.broadcast_to(row.astype(f32), (128, row.shape[1])))[:, :1].astype(i32)


def send_slots(route, peers, slot_count):
    rows = route.shape[1]
    hot = iota((peers, rows), 0) == route
    earlier = ones_where(iota((rows, rows), 0) < iota((rows, rows), 1))
    rank = dot(ones_where(hot), earlier)
    rank = jnp.sum(jnp.where(hot, rank, 0.0), axis=0, keepdims=True)
    return route * slot_count + rank.astype(i32)


def place_rows(count, slots):
    peers = count.shape[0]
    per = slots // peers
    lane = iota((peers, slots), 1)
    low = iota((peers, slots), 0) * per
    mine = (lane >= low) & (lane < low + per)
    before = jnp.sum(jnp.where(lane >= low + per, count, 0.0), axis=0, keepdims=True)
    held = jnp.sum(jnp.where(mine, count, 0.0), axis=0, keepdims=True)
    within = jnp.sum(jnp.where(mine, (lane - low).astype(f32), 0.0), axis=0, keepdims=True)
    return jnp.where(within < held, before + within, -1.0).astype(i32)


def pack_product(planes, route, first, second, slot_count, peers, tile=512):
    _, rows, channels = planes.shape
    slots = peers * slot_count

    def body(route_ref, a_ref, b_ref, out_ref, hot_ref, fill_ref):
        @pl.when(pl.program_id(0) == 0)
        def _():
            hot = ones_where(iota((slots, rows), 0) == send_slots(route_ref[...], peers, slot_count))
            hot_ref[...] = hot
            fill_ref[...] = EMPTY * (1.0 - dot(hot, jnp.ones((rows, 128), bf16)))

        x = (a_ref[0].astype(f32) * b_ref[0].astype(f32)).astype(bf16)
        out_ref[...] = (dot(hot_ref[...], x) + fill_ref[:, :1]).astype(bf16)

    return pl.pallas_call(
        body,
        grid=(channels // tile,),
        in_specs=[whole((1, rows))]
        + [pl.BlockSpec((1, rows, tile), functools.partial(lambda s, j: (s, 0, j), s)) for s in (first, second)],
        out_specs=cols((slots, tile)),
        out_shape=jax.ShapeDtypeStruct((slots, channels), bf16),
        scratch_shapes=[pltpu.VMEM((slots, rows), bf16), pltpu.VMEM((slots, 128), f32)],
        compiler_params=params(),
        cost_estimate=cost(2 * slots * rows * channels, 2 * (2 * rows + slots) * channels),
        name="pack_kv",
    )(in_hbm(route), planes, planes)


def pack_two(planes, route, first, second, slot_count, peers, tile=512):
    _, rows, channels = planes.shape
    slots = peers * slot_count

    def body(route_ref, a_ref, b_ref, out_a_ref, out_b_ref, back_ref, hot_ref):
        @pl.when(pl.program_id(0) == 0)
        def _():
            slot = send_slots(route_ref[...], peers, slot_count)
            hot_ref[...] = ones_where(iota((slots, rows), 0) == slot)
            back_ref[...] = ones_where(iota((rows, slots), 1) == as_column(slot))

        out_a_ref[...] = dot(hot_ref[...], a_ref[0]).astype(bf16)
        out_b_ref[...] = dot(hot_ref[...], b_ref[0]).astype(bf16)

    return pl.pallas_call(
        body,
        grid=(channels // tile,),
        in_specs=[whole((1, rows))]
        + [pl.BlockSpec((1, rows, tile), functools.partial(lambda s, j: (s, 0, j), s)) for s in (first, second)],
        out_specs=[cols((slots, tile)), cols((slots, tile)), whole((rows, slots))],
        out_shape=[
            jax.ShapeDtypeStruct((slots, channels), bf16),
            jax.ShapeDtypeStruct((slots, channels), bf16),
            jax.ShapeDtypeStruct((rows, slots), bf16),
        ],
        scratch_shapes=[pltpu.VMEM((slots, rows), bf16)],
        compiler_params=params(),
        cost_estimate=cost(4 * slots * rows * channels, 4 * (rows + slots) * channels),
        name="pack_two",
    )(in_hbm(route), planes, planes)


def place_matrices(received, rows, slot_count, peers):
    slots = received.shape[0]

    def body(in_ref, to_ref, steps_ref, back_ref):
        used = ones_where(in_ref[...].astype(f32) < 0.75 * EMPTY)
        lane = iota((peers, slots), 1)
        low = iota((peers, slots), 0) * slot_count
        at = place_rows(dot(ones_where((lane >= low) & (lane < low + slot_count)), used)[:, :1], slots)
        to_ref[...] = ones_where(iota((rows, slots), 0) == at)
        span = rows // SEGS
        at = jnp.where(at < 0, at, (at % span) * SEGS + at // span)
        steps_ref[...] = ones_where(iota((rows, slots), 0) == at)
        back_ref[...] = ones_where(iota((slots, rows), 1) == as_column(at))

    return pl.pallas_call(
        body,
        grid=(1,),
        in_specs=[pl.BlockSpec((slots, 128), lambda j: (0, 0))],
        out_specs=[whole((rows, slots)), whole((rows, slots)), whole((slots, rows))],
        out_shape=[
            jax.ShapeDtypeStruct((rows, slots), bf16),
            jax.ShapeDtypeStruct((rows, slots), bf16),
            jax.ShapeDtypeStruct((slots, rows), bf16),
        ],
        compiler_params=params(),
        cost_estimate=cost(1e6, 6 * rows * slots),
        name="place",
    )(received)


def unpack(received, to_rows, tile=512):
    slots, channels = received.shape
    rows = to_rows.shape[0]

    def body(hot_ref, in_ref, out_ref):
        out_ref[...] = dot(hot_ref[...], in_ref[...]).astype(bf16)

    return pl.pallas_call(
        body,
        grid=(channels // tile,),
        in_specs=[whole(to_rows.shape), cols((slots, tile))],
        out_specs=cols((rows, tile)),
        out_shape=jax.ShapeDtypeStruct((rows, channels), bf16),
        compiler_params=params(),
        cost_estimate=cost(2 * slots * rows * channels, 2 * (rows + slots) * channels),
        name="unpack",
    )(to_rows, received)


def finish(returned, planes, plane, back, tile=512):
    slots, channels = returned.shape
    _, rows, _ = planes.shape

    def body(back_ref, gate_ref, in_ref, out_ref):
        out_ref[...] = (gate_ref[0].astype(f32) * dot(back_ref[...], in_ref[...])).astype(bf16)

    return pl.pallas_call(
        body,
        grid=(channels // tile,),
        in_specs=[
            whole((rows, slots)),
            pl.BlockSpec((1, rows, tile), lambda j: (plane, 0, j)),
            cols((slots, tile)),
        ],
        out_specs=cols((rows, tile)),
        out_shape=jax.ShapeDtypeStruct((rows, channels), bf16),
        compiler_params=params(),
        cost_estimate=cost(2 * slots * rows * channels, 2 * (2 * rows + slots) * channels),
        name="finish",
    )(back, planes, returned)


def two_parts(table):
    high = table.astype(ml_dtypes.bfloat16)
    return high, (table - high.astype(np.float64)).astype(ml_dtypes.bfloat16)


def dft_tables(taps):
    points = 2 * taps
    k = np.arange(taps)[:, None].astype(np.float64)
    t = np.arange(points)[None, :].astype(np.float64)
    forward = np.concatenate(
        [np.cos(2 * np.pi * k * t / points), np.cos(np.pi * t), -np.sin(2 * np.pi * k[1:] * t / points)]
    )
    inverse = forward.T[taps:] * (2.0 / points)
    inverse[:, 0] *= 0.5
    inverse[:, taps] *= 0.5
    return np.concatenate(two_parts(forward)), np.concatenate(two_parts(inverse))


def side_by_side(rows):
    p = np.arange(rows)
    t = (p % SEGS) * (rows // SEGS) + p // SEGS
    return (t[:, None] == p[None, :]).astype(ml_dtypes.bfloat16)


def forward_dft(table, x):
    both = dot(table, x)
    half = both.shape[0] // 2
    return both[:half] + both[half:]


def inverse_dft(table, y):
    half = table.shape[0] // 2
    high = y.astype(bf16)
    low = (y - high.astype(f32)).astype(bf16)
    both = dot(table, high)
    return both[:half] + both[half:] + dot(table[:half], low)


def through_filter(spectrum, filter_ref, inverse_table):
    taps = spectrum.shape[0] // 2
    a, b = spectrum[:taps], spectrum[taps:]
    re, im, re_last = filter_ref[0], filter_ref[1], filter_ref[2]
    return inverse_dft(inverse_table, jnp.concatenate([a * re - b * im, a * im + b * re_last]))


def filter_spectrum(mr_filter, forward, tile=512):
    taps, channels = mr_filter.shape

    def body(taps_ref, fwd_ref, out_ref):
        fwd = fwd_ref[:, :taps]
        x = taps_ref[...]
        high = x.astype(bf16)
        low = (x - high.astype(f32)).astype(bf16)
        h = forward_dft(fwd, high) + dot(fwd[: 2 * taps], low)
        first = iota((taps, tile), 0) == 0
        out_ref[0] = h[:taps]
        out_ref[1] = jnp.where(first, 0.0, h[taps:])
        out_ref[2] = jnp.where(first, h[taps:], h[:taps])

    return pl.pallas_call(
        body,
        grid=(channels // tile,),
        in_specs=[cols((taps, tile)), whole(forward.shape)],
        out_specs=cols((3, taps, tile)),
        out_shape=jax.ShapeDtypeStruct((3, taps, channels), f32),
        compiler_params=params(),
        cost_estimate=cost(6 * 2 * taps * taps * channels, 16 * taps * channels),
        name="spectrum",
    )(mr_filter, forward)


def filter_rows(u, spectrum, forward, inverse, tile=512):
    rows, channels = u.shape
    taps = spectrum.shape[1]

    def body(u_ref, h_ref, fwd_ref, inv_ref, out_ref):
        for b in range(rows // taps):
            if b == 0:
                x = forward_dft(fwd_ref[:, taps:], u_ref[:taps])
            else:
                x = forward_dft(fwd_ref[...], u_ref[(b - 1) * taps : (b + 1) * taps])
            out_ref[b * taps : (b + 1) * taps] = through_filter(x, h_ref, inv_ref[...])

    return pl.pallas_call(
        body,
        grid=(channels // tile,),
        in_specs=[cols((rows, tile)), cols((3, taps, tile)), whole(forward.shape), whole(inverse.shape)],
        out_specs=cols((rows, tile)),
        out_shape=jax.ShapeDtypeStruct((rows, channels), f32),
        compiler_params=params(),
        cost_estimate=cost(14 * taps * rows * channels, 8 * rows * channels),
        name="taps",
    )(u, spectrum, forward, inverse)


def gate(received, to_rows, filtered, rim, spectrum, forward, inverse, beside, tile=512):
    slots, channels = received.shape
    rows = to_rows.shape[0]
    taps = spectrum.shape[1]

    def body(hot_ref, in_ref, filt_ref, rim_ref, h_ref, fwd_ref, inv_ref, beside_ref, out_ref):
        q = dot(hot_ref[...], in_ref[...])
        early = through_filter(forward_dft(fwd_ref[:, :taps], rim_ref[...]), h_ref, inv_ref[...])
        first = (q[:taps] * (filt_ref[:taps] + early)).astype(bf16)
        rest = (q[taps:] * filt_ref[taps:]).astype(bf16)
        out_ref[...] = dot(beside_ref[...], jnp.concatenate([first, rest])).astype(bf16)

    return pl.pallas_call(
        body,
        grid=(channels // tile,),
        in_specs=[
            whole(to_rows.shape),
            cols((slots, tile)),
            cols((rows, tile)),
            cols((taps, tile)),
            cols((3, taps, tile)),
            whole(forward.shape),
            whole(inverse.shape),
            whole((rows, rows)),
        ],
        out_specs=cols((rows, tile)),
        out_shape=jax.ShapeDtypeStruct((rows, channels), bf16),
        compiler_params=params(),
        cost_estimate=cost(2 * slots * rows * channels, (6 * rows + 2 * slots) * channels),
        name="gate",
    )(in_hbm(to_rows), in_hbm(received), in_hbm(filtered), rim, spectrum, forward, inverse, in_hbm(beside))


def project(tasks, blocks, own, other, weight, other_weight, tile=512):
    rows, depth = own.shape
    width = depth
    steps = width // tile
    adds = [add for _, _, _, add, _ in tasks if add is not None]
    shapes = [jax.ShapeDtypeStruct((take, width), kind) for _, _, splits, _, kind in tasks for take in splits]

    def body(blocks_ref, own_ref, other_ref, *rest):
        arrived = iter(rest[2 * len(tasks) : 2 * len(tasks) + len(adds)])
        outs = iter(rest[2 * len(tasks) + len(adds) :])
        for n, (_, low, splits, add, kind) in enumerate(tasks):
            at = slice(low, low + sum(splits))
            total = dot(own_ref[at], rest[2 * n][...]) + dot(other_ref[at], rest[2 * n + 1][...])
            if add is not None:
                total = total + next(arrived)[...].astype(f32)
            start = 0
            for take in splits:
                next(outs)[...] = total[start : start + take].astype(kind)
                start += take

    specs = [whole((rows, depth))] * 2
    operands = [own, other]
    for dx, *_ in tasks:
        spec = pl.BlockSpec(
            (depth, tile), functools.partial(lambda d, j, b: (0, b[d] * steps + j), dx)
        )
        specs += [spec, spec]
        operands += [weight, other_weight]
    for add in adds:
        specs.append(cols((add.shape[0], tile)))
        operands.append(add)
    total_rows = sum(shape.shape[0] for shape in shapes)
    return pl.pallas_call(
        body,
        grid_spec=pltpu.PrefetchScalarGridSpec(
            num_scalar_prefetch=1,
            grid=(steps,),
            in_specs=specs,
            out_specs=[cols((shape.shape[0], tile)) for shape in shapes],
        ),
        out_shape=shapes,
        compiler_params=params(),
        cost_estimate=cost(
            4 * depth * width * total_rows, 4 * depth * width * len(tasks) + 4 * rows * depth + 4 * total_rows * width
        ),
        name="project",
    )(blocks, *operands)


def rows_of(t):
    return pl.ds(pl.multiple_of(t * SEGS, SEGS), SEGS)


def spread(ref, which, lanes):
    return [jnp.broadcast_to(ref[which, n : n + 1, lanes], (SEGS, 128)) for n in range(ORDER)]


def total_of(terms):
    while len(terms) > 1:
        terms = [a + b for a, b in zip(terms[::2], terms[1::2])]
    return terms[0]


def end_states(table, own, arrived, k_li, last, coef, peers, tile=256):
    rows, width = own.shape
    half = rows // 2
    blocks = tile // 128

    def body(table_ref, own_ref, a0_ref, a1_ref, b0_ref, b1_ref, k_ref, last_ref, coef_ref, u_ref, seg_ref, end_ref):
        top = own_ref[:half].astype(f32) + a0_ref[...].astype(f32) + a1_ref[...].astype(f32)
        top = top * k_ref[:half].astype(f32)
        bottom = own_ref[half:].astype(f32) + b0_ref[...].astype(f32) + b1_ref[...].astype(f32)
        bottom = bottom * k_ref[half:].astype(f32)
        for cb in range(blocks):
            lanes = slice(cb * 128, (cb + 1) * 128)
            u_ref[cb, :half] = top[:, lanes]
            u_ref[cb, half:] = bottom[:, lanes]
        for cb in range(blocks):
            lanes = slice(cb * 128, (cb + 1) * 128)
            decay = spread(coef_ref, 0, lanes)

            def step(t, state):
                u = u_ref[cb, rows_of(t), :] * last_ref[rows_of(t), :]
                return tuple(d * s + u for d, s in zip(decay, state))

            state = lax.fori_loop(0, rows // SEGS, step, (jnp.zeros((SEGS, 128), f32),) * ORDER, unroll=8)
            for n in range(ORDER):
                seg_ref[cb, n * SEGS : (n + 1) * SEGS] = state[n]
            total = jnp.zeros((ORDER, 128), f32)
            for s in range(SEGS):
                keep = jnp.where(table_ref[s] == 0, coef_ref[1, :, lanes], 0.0)
                total = keep * total + seg_ref[cb, pl.ds(s, ORDER, stride=SEGS), :]
            for p in range(peers):
                end_ref[p * ORDER : (p + 1) * ORDER, lanes] = total.astype(bf16)

    return pl.pallas_call(
        body,
        grid_spec=pltpu.PrefetchScalarGridSpec(
            num_scalar_prefetch=1,
            grid=(width // tile,),
            in_specs=[
                cols((rows, tile)),
                cols((half, tile)),
                cols((half, tile)),
                cols((half, tile)),
                cols((half, tile)),
                cols((rows, tile)),
                whole(last.shape),
                cols((4, ORDER, tile)),
            ],
            out_specs=[
                leading((blocks, rows, 128)),
                leading((blocks, ORDER * SEGS, 128)),
                cols((peers * ORDER, tile)),
            ],
        ),
        out_shape=[
            jax.ShapeDtypeStruct((width // 128, rows, 128), f32),
            jax.ShapeDtypeStruct((width // 128, ORDER * SEGS, 128), f32),
            jax.ShapeDtypeStruct((peers * ORDER, width), bf16),
        ],
        compiler_params=params(),
        cost_estimate=cost(4e9, 12 * rows * width),
        name="ends",
    )(table, own, *arrived, k_li, last, coef)


def recur(table, segs, u, keep, coef, step_blocks=2):
    count, rows, _ = u.shape

    def body(table_ref, seg_ref, u_ref, keep_ref, coef_ref, li_ref, in_ref):
        for cb in range(step_blocks):
            lanes = slice(cb * 128, (cb + 1) * 128)
            enter = jnp.zeros((ORDER, 128), f32)
            for s in range(SEGS):
                in_ref[pl.ds(s, ORDER, stride=SEGS), :] = enter
                fade = jnp.where(table_ref[s] == 0, coef_ref[1, :, lanes], 0.0)
                enter = fade * enter + seg_ref[cb, pl.ds(s, ORDER, stride=SEGS), :]
            decay, weigh = spread(coef_ref, 0, lanes), spread(coef_ref, 3, lanes)

            def step(t, state):
                u, kept = u_ref[cb, rows_of(t), :], keep_ref[rows_of(t), :]
                state = tuple((d * s) * kept + u for d, s in zip(decay, state))
                li_ref[cb, rows_of(t), :] = total_of([w * s for w, s in zip(weigh, state)])
                return state

            state = tuple(in_ref[n * SEGS : (n + 1) * SEGS] for n in range(ORDER))
            lax.fori_loop(0, rows // SEGS, step, state, unroll=8)

    return pl.pallas_call(
        body,
        grid_spec=pltpu.PrefetchScalarGridSpec(
            num_scalar_prefetch=1,
            grid=(count // step_blocks,),
            in_specs=[
                leading((step_blocks, ORDER * SEGS, 128)),
                leading((step_blocks, rows, 128)),
                whole(keep.shape),
                cols((4, ORDER, step_blocks * 128)),
            ],
            out_specs=leading((step_blocks, rows, 128)),
            scratch_shapes=[pltpu.VMEM((ORDER * SEGS, 128), f32)],
        ),
        out_shape=jax.ShapeDtypeStruct(u.shape, f32),
        compiler_params=params(),
        cost_estimate=cost(8e9, 8 * count * rows * 128),
        name="recur",
    )(table, segs, in_hbm(u), keep, coef)


def carry_in(table, ends, li, unbroken, coef, back, peers, step_blocks=4):
    count, rows, _ = li.shape
    slots = back.shape[0]
    tile = step_blocks * 128

    def body(table_ref, ends_ref, li_ref, unbroken_ref, coef_ref, back_ref, out_ref, in_ref, sum_ref):
        def hop(j, carry):
            return jnp.where(table_ref[SEGS + j] == 0, coef_ref[2], 0.0) * carry + ends_ref[j].astype(f32)

        carry = lax.fori_loop(0, table_ref[SEGS + peers], hop, jnp.zeros((ORDER, tile), f32))
        for cb in range(step_blocks):
            lanes = slice(cb * 128, (cb + 1) * 128)
            enter = carry[:, lanes] * coef_ref[3, :, lanes]
            for s in range(SEGS):
                in_ref[pl.ds(s, ORDER, stride=SEGS), :] = enter
                enter = coef_ref[1, :, lanes] * enter
            decay = spread(coef_ref, 0, lanes)

            def step(t, state):
                state = tuple(d * s for d, s in zip(decay, state))
                more = total_of(list(state)) * unbroken_ref[rows_of(t), :]
                sum_ref[rows_of(t), lanes] = li_ref[cb, rows_of(t), :] + more
                return state

            state = tuple(in_ref[n * SEGS : (n + 1) * SEGS] for n in range(ORDER))
            lax.fori_loop(0, rows // SEGS, step, state, unroll=8)
        out_ref[...] = dot(back_ref[...], sum_ref[...].astype(bf16)).astype(bf16)

    return pl.pallas_call(
        body,
        grid_spec=pltpu.PrefetchScalarGridSpec(
            num_scalar_prefetch=1,
            grid=(count // step_blocks,),
            in_specs=[
                cols((peers, ORDER, tile)),
                leading((step_blocks, rows, 128)),
                whole(unbroken.shape),
                cols((4, ORDER, tile)),
                whole(back.shape),
            ],
            out_specs=cols((slots, tile)),
            scratch_shapes=[pltpu.VMEM((ORDER * SEGS, 128), f32), pltpu.VMEM((rows, tile), f32)],
        ),
        out_shape=jax.ShapeDtypeStruct((slots, count * 128), bf16),
        compiler_params=params(),
        cost_estimate=cost(4e9, 8 * count * rows * 128),
        name="carry",
    )(table, ends, li, unbroken, coef, in_hbm(back))


def along_x(shard, dx, dcore=0):
    count = lax.axis_size("tp") // 2
    pairs = [
        (2 * x + c, 2 * ((x + dx) % count) + (c + dcore) % 2) for x in range(count) for c in range(2)
    ]
    return lax.ppermute(shard, "tp", pairs)


def lane_mask(hit):
    return jnp.broadcast_to(jnp.where(hit, 0.0, 1.0).astype(f32)[:, None], (hit.shape[0], 128))


def swap(shard):
    return lax.all_to_all(shard, "ctx", split_axis=0, concat_axis=0, tiled=True)


def together(*arrays):
    return lax.optimization_barrier(arrays)


def on_device(projected, route, contig_len, mr_filter, out_weight, li_rate, li_residue):
    rows, _, channels = projected.shape
    peers = lax.axis_size("ctx")
    slot_count = 3 * rows // (2 * peers)
    taps = mr_filter.shape[0]
    half = rows // 2
    me = lax.axis_index("ctx").astype(i32)
    tp = lax.axis_index("tp").astype(i32)
    chip, core = tp // 2, tp % 2
    chips = lax.axis_size("tp") // 2
    planes = jnp.transpose(projected, (1, 0, 2))
    route_row = route.reshape(1, rows)
    me_row = me.reshape(1)
    span = rows // SEGS
    forward, inverse = (jnp.asarray(t) for t in dft_tables(taps))
    beside = jnp.asarray(side_by_side(rows))

    packed_kv = pack_product(planes, route_row, 1, 2, slot_count, peers)
    packed_kv, other_source = together(packed_kv, out_weight)
    other_weight = along_x(other_source, 0, 1)
    got_kv = swap(packed_kv)
    packed_q, packed_k, to_loader = pack_two(planes, route_row, 0, 4, slot_count, peers)

    order = jnp.arange(contig_len.shape[0], dtype=i32)
    starts = jnp.sum(jnp.where(order[:, None] < order[None, :], contig_len[:, None], 0), axis=0)
    here = me * rows + jnp.arange(SEGS, dtype=i32)[None, :] * span + jnp.arange(span, dtype=i32)[:, None]
    here = here.reshape(rows, 1)
    seg_last = here - here % span + (span - 1)
    seen, behind = starts[None, :] <= here, starts[None, :] > here
    keep = lane_mask(jnp.any(starts[None, :] == here, axis=1))
    last = lane_mask(jnp.any(behind & (starts[None, :] <= seg_last), axis=1))
    unbroken = lane_mask(jnp.any(seen & (starts[None, :] >= me * rows), axis=1))
    seg_ids = me * SEGS + jnp.arange(SEGS, dtype=i32)
    seg_has = jnp.any(seg_ids[:, None] == (starts // span)[None, :], axis=1)
    dev_has = jnp.any(jnp.arange(peers, dtype=i32)[:, None] == (starts // rows)[None, :], axis=1)
    table = jnp.concatenate([seg_has.astype(i32), dev_has.astype(i32), me_row])
    mode_weight = li_residue * jnp.sqrt(-jnp.expm1(-2.0 * li_rate))
    coef = jnp.stack([jnp.exp(-li_rate), jnp.exp(-li_rate * span), jnp.exp(-li_rate * rows), mode_weight])
    spectrum = filter_spectrum(mr_filter, forward)

    blocks = jnp.stack([2 * ((chip + d) % chips) + core for d in range(chips)]).astype(i32)

    got_kv, packed_q, coef, spectrum = together(got_kv, packed_q, coef, spectrum)
    got_q = swap(packed_q)
    to_rows, to_steps, to_slots = place_matrices(got_kv, rows, slot_count, peers)
    u_mr = unpack(got_kv, to_rows)
    rim = lax.ppermute(u_mr[rows - taps :], "ctx", [(i, i + 1) for i in range(peers - 1)])
    filtered = filter_rows(u_mr, spectrum, forward, inverse)
    got_q, filtered, packed_k = together(got_q, filtered, packed_k)
    got_k = swap(packed_k)
    gated = gate(got_q, to_rows, filtered, rim, spectrum, forward, inverse, beside)
    other = along_x(gated, 0, 1)
    mm = functools.partial(project, own=gated, weight=out_weight, other_weight=other_weight)
    far_a, far_b = mm([(2, 0, (half, half), None, bf16)], blocks, other=other)
    blocks, far_a, far_b = together(blocks, far_a, far_b)
    pass_a, pass_b = along_x(far_a, 1), along_x(far_b, -1)
    up_b, down_a = mm([(1, half, (half,), None, bf16), (3, 0, (half,), None, bf16)], blocks, other=other)
    up_b, down_a, blocks = together(up_b, down_a, blocks)
    from_low_b, from_high_a = along_x(up_b, 1), along_x(down_a, -1)
    up_a, down_b = mm([(1, 0, (half,), pass_a, bf16), (3, half, (half,), pass_b, bf16)], blocks, other=other)
    up_a, down_b, blocks, got_k = together(up_a, down_b, blocks, got_k)
    from_low_a, from_high_b = along_x(up_a, 1), along_x(down_b, -1)
    [mine] = mm([(0, 0, (rows,), None, bf16)], blocks, other=other)
    k_li = unpack(got_k, to_steps)
    u, segs, end = end_states(
        table, mine, [from_low_a, from_high_a, from_low_b, from_high_b], k_li, last, coef, peers
    )
    ends = swap(end).reshape(peers, ORDER, channels)
    li = recur(table, segs, u, keep, coef)
    returned = swap(carry_in(table, ends, li, unbroken, coef, to_slots, peers))
    return finish(returned, planes, 3, to_loader)


def solution(mesh):
    return jax.shard_map(
        on_device,
        mesh=mesh,
        in_specs=(
            P("ctx", None, "tp"),
            P("ctx"),
            P(),
            P(None, "tp"),
            P("tp", None),
            P(None, "tp"),
            P(None, "tp"),
        ),
        out_specs=P("ctx", "tp"),
        check_vma=False,
    )
```
